128 devices in a mesh: row: 8 (over z, core), col: 16 (over y, x).
Axes of the slice: x: 4, y: 4, z: 4, core: 2. Of those that a mesh axis runs over, the one named last changes fastest.
Arguments:
- image_embeds: float32 [32768, 512], P(('row', 'col')), may hold values from -60 to 60
- text_embeds: float32 [32768, 512], P(('col', 'row')), may hold values from -60 to 60
- logit_scale: float32 [], replicated, may hold values from 1 to 4
Outputs:
- grad_image: float32 [32768, 512], P(('row', 'col'))
- grad_text: float32 [32768, 512], P(('col', 'row'))
- grad_scale: float32 [], replicated
The draws below stay inside these ranges and needn't reach their ends.
All inputs are finite; a program needn't handle non-finite values.
Results may differ from the reference program's by a relative error of at most 0.0023.
The reference program's roundings to bfloat16 on the way (of `image_half`, `text_half` and `grad_half`) count: a program that leaves them out, or rounds other values in their place, can miss the bound.
Values may be sent and summed in bfloat16 or wider, within the bound.
A program may use at most 128 MiB of HBM per device.

```python
import math
import jax
import jax.numpy as jnp
from jax import lax

E = 512
BATCH = 32768


def draw_image_embeds(key, part):
    key = jax.random.fold_in(key, 11)
    first_key, second_key = jax.random.split(key)
    noise = jax.random.normal(first_key, (BATCH, E), jnp.float32) * E ** (-0.25)
    factor = jnp.exp(jax.random.uniform(second_key, (BATCH, 1), jnp.float32, math.log(0.5), math.log(2.5)))
    values = factor * noise
    return jnp.clip(values, -60.0, 60.0)


def draw_text_embeds(key, part):
    key = jax.random.fold_in(key, 23)
    first_key, second_key = jax.random.split(key)
    noise = jax.random.normal(first_key, (BATCH, E), jnp.float32) * E ** (-0.25)
    factor = jnp.exp(jax.random.uniform(second_key, (BATCH, 1), jnp.float32, math.log(0.5), math.log(2.5)))
    values = factor * noise
    return jnp.clip(values, -60.0, 60.0)


def setup_inputs(seed: int = 0) -> dict:
    seeds = jax.random.split(jax.random.key(seed), 4)
    return {
        "image_embeds": draw_image_embeds(jax.random.fold_in(seeds[3], 71), 0),
        "text_embeds": draw_text_embeds(jax.random.fold_in(seeds[3], 71), 0),
        "logit_scale": jnp.clip(jnp.exp(jax.random.uniform(seeds[2], (), jnp.float32, math.log(1.0), math.log(4.0))), 1.0, 4.0),
    }


def reference(image_embeds, text_embeds, logit_scale):
    image_half = image_embeds.astype(jnp.bfloat16)
    text_half = text_embeds.astype(jnp.bfloat16)
    block_size = math.gcd(BATCH, 1024)
    blocks = BATCH // block_size
    image_blocks = image_half.reshape(blocks, block_size, E)

    def stats(state, block_rows):
        col_max, col_sum = state
        inner = jnp.dot(block_rows, text_half.T, preferred_element_type=jnp.float32)
        logits = logit_scale * inner
        row_max = jnp.max(logits, axis=1)
        row_lse = row_max + jnp.log(jnp.sum(jnp.exp(logits - row_max[:, None]), axis=1))
        merged = jnp.maximum(col_max, jnp.max(logits, axis=0))
        col_sum = col_sum * jnp.exp(col_max - merged) + jnp.sum(jnp.exp(logits - merged[None, :]), axis=0)
        return (merged, col_sum), row_lse

    start_state = (jnp.full((BATCH,), -1e30, jnp.float32), jnp.zeros((BATCH,), jnp.float32))
    (col_max, col_sum), row_lse = lax.scan(stats, start_state, image_blocks)
    row_lse = row_lse.reshape(blocks, block_size)
    col_lse = col_max + jnp.log(col_sum)
    starts = jnp.arange(blocks, dtype=jnp.int32) * block_size
    columns = jnp.arange(BATCH, dtype=jnp.int32)

    def grads(state, inputs):
        text_acc, scale_acc = state
        block_rows, lse_rows, start = inputs
        inner = jnp.dot(block_rows, text_half.T, preferred_element_type=jnp.float32)
        logits = logit_scale * inner
        matched = ((start + jnp.arange(block_size, dtype=jnp.int32))[:, None] == columns[None, :]).astype(jnp.float32)
        logit_grad = 0.5 * jnp.exp(logits - lse_rows[:, None]) + 0.5 * jnp.exp(logits - col_lse[None, :]) - matched
        scale_acc = scale_acc + jnp.sum(logit_grad * inner)
        grad_half = logit_grad.astype(jnp.bfloat16)
        image_part = logit_scale * jnp.dot(grad_half, text_half, preferred_element_type=jnp.float32)
        text_acc = text_acc + logit_scale * jnp.dot(grad_half.T, block_rows, preferred_element_type=jnp.float32)
        return (text_acc, scale_acc), image_part

    start_grads = (jnp.zeros((BATCH, E), jnp.float32), jnp.zeros((), jnp.float32))
    (grad_text, grad_scale), grad_image = lax.scan(grads, start_grads, (image_blocks, row_lse, starts))
    return grad_image.reshape(BATCH, E), grad_text, grad_scale
```

```python
import functools

import jax
import jax.numpy as jnp
from jax import lax
from jax.experimental import pallas as pl
from jax.experimental.pallas import tpu as pltpu
from jax.sharding import PartitionSpec as P

MESH = pl.DeviceIdType.MESH
NT = (((1,), (1,)), ((), ()))
TN = (((0,), (0,)), ((), ()))
LOG2E = 1.4426950408889634
B = 256
E = 512
H = B // 2
KEPT = 6

IMG = ((0, 0), (0, 1), (1, 0), (3, 0), (2, 0), (1, 1), (3, 1), (2, 1))
TXT = ((0, 0), (0, 1), (1, 0), (3, 0), (1, 1), (3, 1), (2, 0), (2, 1))
TEXT_ORDER = (7, 5, 4, 6, 3, 2, 1, 0)

GI, GT, SIB, RI, RT, DD = 0, 14, 28, 36, 49, 62
ROWS, COLS, SC1, SC2, CHANNELS = 70, 86, 94, 110, 118


def look_up(i, values):
    return sum(v * (i == n).astype(jnp.int32) for n, v in enumerate(values) if v)


def slot_ring(i, slots):
    return look_up(i, [d for d, _ in slots])


def slot_pair(i, slots):
    return look_up(i, [d for _, d in slots])


def text_slot(ring, pair):
    return sum(
        s * ((ring == d) & (pair == e)).astype(jnp.int32)
        for s, (d, e) in enumerate(TXT)
        if s
    )


def kernel(
    scale_ref, img_hbm, txt_hbm, gi_hbm, gt_hbm, gs_ref,
    I, T, LE, LO, TME, TMO, CME, CMO, GE, GO, MS, PB, XS, FR, XR, AR, FRT, XRT, ART,
    MC, SC, RSEND, RRECV, CSEND, CRECV, RLSE, CLSE, ACC, SR1, SR2,
    SS, RS, LS,
):
    f32, bf16 = jnp.float32, jnp.bfloat16
    r, c = lax.axis_index("row"), lax.axis_index("col")
    z, k = r // 2, r % 2
    y, x = c // 4, c % 4
    b = y // 2
    a = (y + b) % 2
    L, TM, CM, G = (LE, LO), (TME, TMO), (CME, CMO), (GE, GO)

    def dev(dx=0, da=0, dk=0, dz=0, db=0):
        xx, zz, kk = (x + dx) % 4, (z + dz) % 4, (k + dk) % 2
        aa, bb = (a + da) % 2, (b + db) % 2
        yy = aa + bb * (3 - 2 * aa)
        return (zz * 2 + kk, yy * 4 + xx)

    def chan(n, src, dst, to):
        return pltpu.make_async_remote_copy(
            src_ref=src, dst_ref=dst, send_sem=SS.at[n], recv_sem=RS.at[n],
            device_id=to, device_id_type=MESH,
        )

    row_peers = [(dx, da, dk) for dk in (0, 1) for da in (0, 1) for dx in range(4) if (dx, da, dk) != (0, 0, 0)]
    col_peers = [(dz, db) for db in (0, 1) for dz in range(4) if (dz, db) != (0, 0)]

    load_i = pltpu.make_async_copy(img_hbm, LE.at[0:B, 0:E], LS.at[0])
    load_t = pltpu.make_async_copy(txt_hbm, LO.at[0:B, 0:E], LS.at[1])
    load_i.start()
    load_t.start()

    barrier = pltpu.get_barrier_semaphore()
    near = [dev(dx=1), dev(dx=3), dev(da=1), dev(dz=1), dev(dz=3), dev(db=1), dev(dk=1)]
    for to in near:
        pl.semaphore_signal(barrier, inc=1, device_id=to, device_id_type=MESH)

    scale = scale_ref[0]
    c2 = scale * LOG2E
    load_i.wait()
    I[0:B, :] = LE[0:B, 0:E].astype(bf16)
    load_t.wait()
    T[0:B, :] = LO[0:B, 0:E].astype(bf16)
    MC[...] = jnp.full(MC.shape, -1e30, f32)
    SC[...] = jnp.zeros(SC.shape, f32)
    MS[:, :, 0:B] = jnp.full((8, B, B), -1e30, f32)
    MS[:, :, B : 2 * B] = jnp.zeros((8, B, B), f32)
    ACC[...] = jnp.zeros(ACC.shape, f32)
    pl.semaphore_wait(barrier, len(near))

    def gather(base, buf, step, slots, plus, minus, partner):
        def at(place, h):
            lo = slots.index(place) * step * B + h * H
            return buf.at[lo : lo + H]

        plan = [
            ("own", (0, 0), partner, (0, 1), (0, 1)),
            ("own", (0, 0), plus, (3, 0), (0, 1)),
            ("own", (0, 0), minus, (1, 0), (1, 0)),
            ("pair", (0, 1), plus, (3, 1), (0, 1)),
            ("pair", (0, 1), minus, (1, 1), (1, 0)),
            ("on", (3, 0), plus, (2, 0), (0,)),
            ("on", (1, 0), minus, (2, 0), (1,)),
            ("on", (3, 1), plus, (2, 1), (0,)),
            ("on", (1, 1), minus, (2, 1), (1,)),
        ]
        out, n = {}, base
        for _, src, to, dst, halves in plan:
            for h in halves:
                out[dst, h, src] = chan(n, at(src, h), at(dst, h), to)
                n += 1
        return out

    xp, xm, pa = dev(dx=1), dev(dx=3), dev(da=1)
    zp, zm, pb = dev(dz=1), dev(dz=3), dev(db=1)
    sib = dev(dk=1)
    gi = gather(GI, I, 2, IMG, xp, xm, pa)
    gt = gather(GT, T, 1, TXT, zp, zm, pb)
    sb = {
        p: chan(SIB + s, I.at[2 * s * B : (2 * s + 1) * B], I.at[(2 * s + 1) * B : (2 * s + 2) * B], sib)
        for s, p in enumerate(IMG)
    }

    def come(cps, dst, h):
        for (to, half, _), cp in cps.items():
            if (to, half) == (dst, h):
                cp.wait_recv()

    for first in (True, False):
        for dst, hh in (((0, 1), (0, 1)), ((3, 0), (0, 1)), ((1, 0), (1, 0))):
            h = hh[0] if first else hh[1]
            gi[dst, h, (0, 0)].start()
            gt[dst, h, (0, 0)].start()
    sb[0, 0].start()

    def logit_tile(i, jp, e):
        xt = lax.dot_general(
            I[pl.ds(pl.multiple_of(i * 2 * B, 2 * B), 2 * B), :],
            T[pl.ds(pl.multiple_of(jp * 2 * B + e * B, B), B), :],
            NT, preferred_element_type=f32,
        )
        return xt * c2

    def lrow(i):
        return pl.multiple_of(jnp.minimum(i, KEPT - 1) * 2 * B, 2 * B)

    def mm_section(i, jp, e):
        xt = logit_tile(i, jp, e)
        L[e][pl.ds(lrow(i), 2 * B), pl.ds(pl.multiple_of(jp * B, B), B)] = xt
        TM[e][...] = jnp.maximum(xt[:, :128], xt[:, 128:])
        CM[e][...] = jnp.max(xt.reshape(2 * B // 8, 8, B), axis=0)

    def st_section(i, jp, e):
        cols = pl.ds(pl.multiple_of(jp * 2 * B + e * B, B), B)
        old = MC[:, cols]
        mc = jnp.maximum(old, CM[e][...])
        MC[:, cols] = mc
        acc = SC[:, cols] * jnp.exp2(old - mc)
        U = 64
        for q in (0, 1):
            for u in range(B // U):
                l = L[e][pl.ds(lrow(i) + q * B + u * U, U), pl.ds(pl.multiple_of(jp * B, B), B)]
                rows, mcol, scol = slice(u * U, (u + 1) * U), slice(q * 128, (q + 1) * 128), slice(B + q * 128, B + (q + 1) * 128)
                old = MS[i, rows, mcol]
                m = jnp.maximum(old, TM[e][q * B + u * U : q * B + (u + 1) * U])
                MS[i, rows, mcol] = m
                MS[i, rows, scol] = (
                    MS[i, rows, scol] * jnp.exp2(old - m) + jnp.exp2(l[:, :128] - m) + jnp.exp2(l[:, 128:] - m)
                )
                acc = acc + jnp.sum(jnp.exp2(l.reshape(U // 8, 8, B) - mc[None]), axis=0)
        SC[:, cols] = acc

    def body(i, jp, prev):
        st_section(prev[0], prev[1], 1)
        mm_section(i, jp, 0)
        st_section(i, jp, 0)
        mm_section(i, jp, 1)
        return (i, jp)

    def sweep(n, index, prev):
        def one(t, carry):
            i, jp = index(t)
            return body(i, jp, carry)

        return lax.fori_loop(0, n, one, prev)

    for cps in (gi, gt):
        come(cps, (0, 1), 0)
        cps[(3, 1), 0, (0, 1)].start()
    for cps in (gi, gt):
        come(cps, (0, 1), 1)
        cps[(1, 1), 1, (0, 1)].start()
        cps[(3, 1), 1, (0, 1)].start()
        cps[(1, 1), 0, (0, 1)].start()
    for cps in (gi, gt):
        come(cps, (3, 0), 0)
        cps[(2, 0), 0, (3, 0)].start()
        come(cps, (1, 0), 1)
        cps[(2, 0), 1, (1, 0)].start()
    sb[0, 1].start()
    for cps in (gi, gt):
        come(cps, (3, 0), 1)
        come(cps, (1, 0), 0)
    sb[3, 0].start()
    sb[1, 0].start()
    for p in ((0, 0), (0, 1), (3, 0), (1, 0)):
        sb[p].wait_recv()

    zero = jnp.int32(0)
    mm_section(zero, zero, 0)
    st_section(zero, zero, 0)
    mm_section(zero, zero, 1)
    prev = (zero, zero)
    prev = sweep(7, lambda t: ((t + 1) // 2, (t + 1) % 2), prev)

    for cps in (gi, gt):
        come(cps, (3, 1), 0)
        cps[(2, 1), 0, (3, 1)].start()
        come(cps, (1, 1), 1)
        cps[(2, 1), 1, (1, 1)].start()
    for cps in (gi, gt):
        come(cps, (3, 1), 1)
        come(cps, (1, 1), 0)
    sb[3, 1].start()
    sb[1, 1].start()
    prev = sweep(4, lambda t: (t, zero + 2), prev)
    sb[3, 1].wait_recv()
    sb[1, 1].wait_recv()
    prev = sweep(6, lambda t: (5 + t // 3, t % 3), prev)

    come(gi, (2, 0), 0)
    come(gi, (2, 0), 1)
    sb[2, 0].start()
    sb[2, 0].wait_recv()
    prev = sweep(3, lambda t: (zero + 4, t), prev)
    for p in ((2, 0), (2, 1)):
        for h in (0, 1):
            come(gt, p, h)
    come(gi, (2, 1), 0)
    come(gi, (2, 1), 1)
    sb[2, 1].start()
    prev = sweep(7, lambda t: (t, zero + 3), prev)
    sb[2, 1].wait_recv()
    prev = sweep(4, lambda t: (zero + 7, t), prev)
    st_section(prev[0], prev[1], 1)

    eye = lax.broadcasted_iota(jnp.int32, (128, 128), 0) == lax.broadcasted_iota(jnp.int32, (128, 128), 1)

    def image_block(i, q):
        return ((k + q) % 2) * 8 + ((a + slot_pair(i, IMG)) % 2) * 4 + (x + slot_ring(i, IMG)) % 4

    def text_block(j):
        return ((b + slot_pair(j, TXT)) % 2) * 4 + (z + slot_ring(j, TXT)) % 4

    def row_lse(i, carry):
        for q in (0, 1):
            m = MS[i, :, q * 128 : (q + 1) * 128]
            s = MS[i, :, B + q * 128 : B + (q + 1) * 128]
            mr = jnp.max(m, axis=1, keepdims=True)
            lse = mr + jnp.log2(jnp.sum(s * jnp.exp2(m - mr), axis=1, keepdims=True))
            for h in (0, 1):
                v = jnp.broadcast_to(lse[h * 128 : (h + 1) * 128], (128, 128))
                RSEND[pl.ds(image_block(i, q) * 2 + h, 1), :] = jnp.sum(jnp.where(eye, v, 0.0), axis=0, keepdims=True)
        return carry

    lax.fori_loop(0, 8, row_lse, 0)
    rows_out = []
    for dx, da, dk in row_peers:
        to, here = dk * 8 + da * 4 + dx, dk * 8 + da * 4 + (4 - dx) % 4
        rows_out.append(chan(ROWS + here, RSEND, RRECV.at[here], dev(dx=dx, da=da, dk=dk)))
        rows_out[-1].start()
    mc = MC[...]
    mr = jnp.max(mc, axis=0, keepdims=True)
    lse = mr + jnp.log2(jnp.sum(SC[...] * jnp.exp2(mc - mr), axis=0, keepdims=True))
    for j in range(8):
        for h in (0, 1):
            CSEND[pl.ds(text_block(jnp.int32(j)) * 2 + h, 1), :] = lse[:, j * B + h * 128 : j * B + (h + 1) * 128]
    cols_out = []
    for dz, db in col_peers:
        here = db * 4 + (4 - dz) % 4
        cols_out.append(chan(COLS + here, CSEND, CRECV.at[here], dev(dz=dz, db=db)))
        cols_out[-1].start()

    for cp in cols_out:
        cp.wait_recv()
    parts = [CSEND[...]] + [CRECV[n] for n in range(1, 8)]
    m = functools.reduce(jnp.maximum, parts)
    CLSE[...] = m + 1.0 + jnp.log2(sum(jnp.exp2(v - m) for v in parts))
    for j in range(8):
        for h in (0, 1):
            MC[:, j * B + h * 128 : j * B + (h + 1) * 128] = jnp.broadcast_to(
                CLSE[pl.ds(text_block(jnp.int32(j)) * 2 + h, 1), :], (8, 128)
            )
    for cp in rows_out:
        cp.wait_recv()
    parts = [RSEND[...]] + [RRECV[n] for n in range(1, 16)]
    m = functools.reduce(jnp.maximum, parts)
    RLSE[...] = m + 1.0 + jnp.log2(sum(jnp.exp2(v - m) for v in parts))

    for cp in [*gi.values(), *gt.values(), *sb.values()]:
        cp.wait_send()

    def row_col(i, q, h):
        v = RLSE[pl.ds(image_block(i, q) * 2 + h, 1), :]
        v = jnp.sum(jnp.where(eye, jnp.broadcast_to(v, (128, 128)), 0.0), axis=1, keepdims=True)
        return jnp.broadcast_to(v, (128, 128))

    def grow(i):
        return pl.multiple_of((i // 2) * 2 * B, 2 * B)

    def grads(i, e):
        U = 32
        acc = ACC[...]
        for q in (0, 1):
            for h in (0, 1):
                rl = row_col(i, q, h)
                for u in range(128 // U):
                    off = q * B + h * 128 + u * U
                    rb = rl[u * U : (u + 1) * U]
                    rb = jnp.concatenate([rb, rb], axis=1)
                    for j in range(8):
                        l = L[j % 2][pl.ds(lrow(i) + off, U), (j // 2) * B : (j // 2 + 1) * B]
                        cl = MC[:, j * B : (j + 1) * B]
                        g = jnp.exp2(l - rb) + jnp.exp2(l.reshape(U // 8, 8, B) - cl[None]).reshape(U, B)
                        w = jnp.sum((g * l).reshape(U // 8, 8, B), axis=0)
                        acc = acc + w[:, :128] + w[:, 128:]
                        G[e][pl.ds(grow(i) + off, U), j * B : (j + 1) * B] = g.astype(bf16)
        ACC[...] = acc

    def matched(i, par):
        ai, xi = (a + slot_pair(i, IMG)) % 2, (x + slot_ring(i, IMG)) % 4
        yi = ai + b * (3 - 2 * ai)
        here = (x % 2 == b) & ((z + z // 2) % 2 == a) & (xi % 2 == k)
        j = text_slot((2 * (yi % 2) + xi // 2 - z + 4) % 4, (z // 2 + b) % 2)
        for q in (0, 1):
            for e in (0, 1):

                @pl.when(here & ((k + q) % 2 == x // 2) & (j % 2 == e))
                def _():
                    for h in (0, 1):
                        rows = q * B + h * 128
                        l = L[e][pl.ds(lrow(i) + rows, 128), pl.ds(pl.multiple_of((j // 2) * B + h * 128, 128), 128)]
                        cl = MC[0:1, pl.ds(pl.multiple_of(j * B + h * 128, 128), 128)]
                        g = jnp.exp2(l - row_col(i, q, h)) + jnp.exp2(l - cl)
                        g = jnp.where(eye, g - 1.0, g)
                        G[par][
                            pl.ds(grow(i) + rows, 128),
                            pl.ds(pl.multiple_of(j * B + h * 128, 128), 128),
                        ] = g.astype(bf16)
                        w = jnp.where(eye, l, 0.0)
                        ACC[...] -= jnp.sum(w.reshape(16, 8, 128), axis=0)

    def image_product(i, e):
        p = jnp.dot(G[e][pl.ds(grow(i), 2 * B), :], T[...], preferred_element_type=f32)
        PB[e, 0] = p[:B]
        PB[e, 1] = p[B:]

    def scatter(base, src, own, fr, xr, ar, plus, minus, partner):
        out = {}
        for n, p in enumerate((1, 0)):
            s, lo, hi = base + 6 * n, slice(0, H), slice(H, B)
            out[2, p, 0] = chan(s + 0, src((2, p)).at[lo], fr.at[p, 0], plus)
            out[2, p, 1] = chan(s + 1, src((2, p)).at[hi], fr.at[p, 1], minus)
            out[1, p, 0] = chan(s + 2, src((1, p)).at[lo], xr.at[0, p, lo], plus)
            out[1, p, 1] = chan(s + 3, src((1, p)).at[hi], xr.at[0, p, hi], plus)
            out[3, p, 0] = chan(s + 4, src((3, p)).at[lo], xr.at[1, p, lo], minus)
            out[3, p, 1] = chan(s + 5, src((3, p)).at[hi], xr.at[1, p, hi], minus)
        out[0, 1] = chan(base + 12, own, ar, partner)
        return out

    stage = {(2, 1): 0, (3, 1): 1, (1, 1): 2, (2, 0): 3, (3, 0): 0, (1, 0): 1}
    xs = lambda place: XS.at[stage[place]]
    ts = lambda place: T.at[TXT.index(place) * B : (TXT.index(place) + 1) * B]
    ltext = lambda s: LE.at[s * B : (s + 1) * B, 0:E]
    ri = scatter(RI, xs, MS.at[1], FR, XR, AR, xp, xm, pa)
    rt = scatter(RT, ts, ltext(1), FRT, XRT, ART, zp, zm, pb)

    def across(i, e):
        return chan(DD + i, PB.at[e, 1], MS.at[i], sib)

    def half(h):
        return pl.ds(h * H, H)

    def send_far(cps, place, p, stage_ref):
        stage_ref[...] = p[...].astype(bf16)
        cps[(*place, 0)].start()
        cps[(*place, 1)].start()

    mixed = {1: 0, 3: 1}

    def send_pure(cps, place, p, stage_ref):
        h = 1 - mixed[place[0]]
        stage_ref[half(h)] = p[half(h)].astype(bf16)
        cps[(*place, h)].start()

    def send_mixed(cps, place, p, stage_ref, fr):
        h = mixed[place[0]]
        cps[2, place[1], h].wait_recv()
        stage_ref[half(h)] = (p[half(h)] + fr[place[1], h].astype(f32)).astype(bf16)
        cps[(*place, h)].start()

    def arrived(cps, pair):
        for ring in (1, 3):
            for h in (0, 1):
                cps[ring, pair, h].wait_recv()

    def send_pair(cps, p, xr):
        arrived(cps, 1)
        p[...] += xr[0, 1].astype(f32) + xr[1, 1].astype(f32)
        cps[0, 1].start()

    frees = {(3, 0): (2, 1), (1, 0): (3, 1)}
    waited = [(*frees[p], h) for p in frees for h in (0, 1)]

    def image_sum(s):
        place = IMG[s]
        across(s, s % 2).wait_recv()
        MS[s] += PB[s % 2, 0]
        if place in frees:
            for h in (0, 1):
                ri[(*frees[place], h)].wait_send()
        if place[0] == 2:
            send_far(ri, place, MS.at[s], xs(place))
        elif place[0]:
            send_pure(ri, place, MS.at[s], xs(place))
        across(s, s % 2).wait_send()

    def image_mixed(place):
        send_mixed(ri, place, MS.at[IMG.index(place)], xs(place), FR)

    def again(i):
        @pl.when((i >= KEPT - 1) & (i < 7))
        def _():
            for e in (0, 1):
                for jp in range(4):
                    L[e][(KEPT - 1) * 2 * B : KEPT * 2 * B, jp * B : (jp + 1) * B] = logit_tile(i, jp, e)

    def g_half(i, e):
        again(i)
        grads(i, e)
        image_product(i + 1, 1 - e)
        matched(i, e)
        across(i + 1, 1 - e).start()
        for s in range(7, 1, -1):
            if s % 2 == e:

                @pl.when(i + 2 == s)
                def _():
                    image_sum(s)

    def g_step(t, carry):
        g_half(6 - 2 * t, 0)

        @pl.when(t == 2)
        def _():
            image_mixed((3, 1))
            image_mixed((1, 1))

        g_half(5 - 2 * t, 1)
        return carry

    seven = jnp.int32(7)
    grads(seven, 1)
    matched(seven, 1)
    lax.fori_loop(0, 3, g_step, 0)
    g_half(zero, 0)

    sc1_out = []
    mine = image_block(zero, 0)
    SR1[mine] = ACC[...]
    for dx, da, dk in row_peers:
        here = dk * 8 + da * 4 + (4 - dx) % 4
        sc1_out.append(chan(SC1 + here, ACC, SR1.at[mine], dev(dx=dx, da=da, dk=dk)))
        sc1_out[-1].start()

    image_product(zero, 0)
    across(zero, 0).start()

    mine_t = text_block(zero)
    sc2_out = [
        chan(SC2 + db * 4 + (4 - dz) % 4, ACC, SR2.at[mine_t], dev(dz=dz, db=db)) for dz, db in col_peers
    ]

    def text_send(kind, place, *more):
        kind(rt, place, ltext(TXT.index(place)), ts(place), *more)

    def text_step(t, carry):
        j = look_up(t, TEXT_ORDER)
        cols = pl.ds(pl.multiple_of(j * B, B), B)
        p = None
        for s in range(8):
            v = lax.dot_general(
                G[s % 2][(s // 2) * 2 * B : (s // 2 + 1) * 2 * B, cols],
                I[s * 2 * B : (s + 1) * 2 * B, :],
                TN, preferred_element_type=f32,
            )
            p = v if p is None else p + v
        LE[pl.ds(pl.multiple_of(j * B, B), B), 0:E] = p

        @pl.when(t == 0)
        def _():
            text_send(send_far, (2, 1))
            image_sum(1)
            image_sum(0)
            image_mixed((3, 0))
            image_mixed((1, 0))

        @pl.when(t == 1)
        def _():
            text_send(send_pure, (3, 1))

        @pl.when(t == 2)
        def _():
            text_send(send_pure, (1, 1))

        @pl.when(t == 3)
        def _():
            text_send(send_mixed, (3, 1), FRT)
            text_send(send_mixed, (1, 1), FRT)
            text_send(send_far, (2, 0))

        @pl.when(t == 4)
        def _():
            text_send(send_pure, (3, 0))
            send_pair(ri, MS.at[1], XR)

        @pl.when(t == 5)
        def _():
            text_send(send_pure, (1, 0))
            for cp in sc1_out:
                cp.wait()
            ACC[...] = sum(SR1[n] for n in range(16))
            SR2[mine_t] = ACC[...]
            for cp in sc2_out:
                cp.start()

        @pl.when(t == 7)
        def _():
            text_send(send_mixed, (3, 0), FRT)
            text_send(send_mixed, (1, 0), FRT)

        return carry

    lax.fori_loop(0, 8, text_step, 0)

    def finish(cps, p, xr, ar, out, sem):
        arrived(cps, 0)
        p[...] += xr[0, 0].astype(f32) + xr[1, 0].astype(f32)
        cps[0, 1].wait_recv()
        p[...] = scale * (p[...] + ar[...])
        store = pltpu.make_async_copy(p, out, sem)
        store.start()
        return store

    send_pair(rt, ltext(1), XRT)
    for cp in sc2_out:
        cp.wait()
    gs_ref[0, 0] = jnp.sum(sum(SR2[n] for n in range(8))) / c2
    store_i = finish(ri, MS.at[0], XR, AR, gi_hbm, LS.at[0])
    store_t = finish(rt, ltext(0), XRT, ART, gt_hbm, LS.at[1])

    for cp in rows_out + cols_out:
        cp.wait_send()
    for name, cp in ri.items():
        if name not in waited:
            cp.wait_send()
    for cp in rt.values():
        cp.wait_send()
    store_i.wait()
    store_t.wait()


def on_device(image_embeds, text_embeds, logit_scale):
    f32, bf16 = jnp.float32, jnp.bfloat16
    any_space = pl.BlockSpec(memory_space=pl.ANY)
    smem = pl.BlockSpec(memory_space=pltpu.SMEM)
    grad_image, grad_text, grad_scale = pl.pallas_call(
        kernel,
        out_shape=(
            jax.ShapeDtypeStruct((B, E), f32),
            jax.ShapeDtypeStruct((B, E), f32),
            jax.ShapeDtypeStruct((1, 1), f32),
        ),
        in_specs=[smem, any_space, any_space],
        out_specs=(any_space, any_space, smem),
        scratch_shapes=[
            pltpu.VMEM((16 * B, E), bf16),
            pltpu.VMEM((8 * B, E), bf16),
            pltpu.VMEM((KEPT * 2 * B, 4 * B), f32),
            pltpu.VMEM((KEPT * 2 * B, 4 * B), f32),
            pltpu.VMEM((2 * B, 128), f32),
            pltpu.VMEM((2 * B, 128), f32),
            pltpu.VMEM((8, B), f32),
            pltpu.VMEM((8, B), f32),
            pltpu.VMEM((8 * B, 8 * B), bf16),
            pltpu.VMEM((8 * B, 8 * B), bf16),
            pltpu.VMEM((8, B, E), f32),
            pltpu.VMEM((2, 2, B, E), f32),
            pltpu.VMEM((4, B, E), bf16),
            pltpu.VMEM((2, 2, H, E), bf16),
            pltpu.VMEM((2, 2, B, E), bf16),
            pltpu.VMEM((B, E), f32),
            pltpu.VMEM((2, 2, H, E), bf16),
            pltpu.VMEM((2, 2, B, E), bf16),
            pltpu.VMEM((B, E), f32),
            pltpu.VMEM((8, 8 * B), f32),
            pltpu.VMEM((8, 8 * B), f32),
            pltpu.VMEM((32, 128), f32),
            pltpu.VMEM((16, 32, 128), f32),
            pltpu.VMEM((16, 128), f32),
            pltpu.VMEM((8, 16, 128), f32),
            pltpu.VMEM((32, 128), f32),
            pltpu.VMEM((16, 128), f32),
            pltpu.VMEM((8, 128), f32),
            pltpu.VMEM((16, 8, 128), f32),
            pltpu.VMEM((8, 8, 128), f32),
            pltpu.SemaphoreType.DMA((CHANNELS,)),
            pltpu.SemaphoreType.DMA((CHANNELS,)),
            pltpu.SemaphoreType.DMA((2,)),
        ],
        compiler_params=pltpu.CompilerParams(
            collective_id=0, has_side_effects=True, vmem_limit_bytes=64 << 20
        ),
        cost_estimate=pl.CostEstimate(flops=6 * 4096 * 2048 * 512, bytes_accessed=4 << 20, transcendentals=4 * 4096 * 2048),
    )(logit_scale.reshape(1), image_embeds, text_embeds)
    return grad_image, grad_text, grad_scale.reshape(())


def solution(mesh):
    return jax.shard_map(
        on_device,
        mesh=mesh,
        in_specs=(P(("row", "col"), None), P(("col", "row"), None), P()),
        out_specs=(P(("row", "col"), None), P(("col", "row"), None), P()),
        check_vma=False,
    )
```

```python
import functools

import jax
import jax.numpy as jnp
from jax import lax
from jax.experimental import pallas as pl
from jax.experimental.pallas import tpu as pltpu
from jax.sharding import PartitionSpec as P

MESH = pl.DeviceIdType.MESH
NT = (((1,), (1,)), ((), ()))
TN = (((0,), (0,)), ((), ()))
LOG2E = 1.4426950408889634
B = 256
E = 512
H = B // 2
W = E // 2
KEPT = 7

IMG = ((0, 0), (0, 1), (1, 0), (3, 0), (2, 0), (1, 1), (3, 1), (2, 1))
TXT = ((0, 0), (0, 1), (1, 0), (3, 0), (1, 1), (3, 1), (2, 0), (2, 1))
TEXT_ORDER = (7, 5, 4, 6, 3, 2, 1, 0)
UNITS = (
    (0, 0, 2, 2, 0, 2, 5, 5, 5, 4, 4, 4, 0, 2, 5, 4),
    (1, 1, 3, 3, 1, 3, 6, 6, 6, 7, 7, 7, 1, 3, 6, 7),
    (0, 1, 0, 1, 2, 2, 0, 1, 2, 0, 1, 2, 3, 3, 3, 3),
)

GI, GT, SIB, RI, RT, DD = 0, 14, 28, 36, 50, 64
ROWS, COLS, SC1, SC2, CHANNELS = 72, 88, 96, 112, 120


def look_up(i, values):
    return sum(v * (i == n).astype(jnp.int32) for n, v in enumerate(values) if v)


def slot_ring(i, slots):
    return look_up(i, [d for d, _ in slots])


def slot_pair(i, slots):
    return look_up(i, [d for _, d in slots])


def text_slot(ring, pair):
    return sum(
        s * ((ring == d) & (pair == e)).astype(jnp.int32)
        for s, (d, e) in enumerate(TXT)
        if s
    )


def kernel(
    scale_ref, img_hbm, txt_hbm, gi_hbm, gt_hbm, gs_ref,
    I, T, LE, LO, TME, TMO, CME, CMO, GE, GO, MS, PB, XS, TS, PS, PST, FR, XR, AR, ARH, FRT, XRT, ART, ARHT,
    MC, SC, RSEND, RRECV, CSEND, CRECV, RLSE, CLSE, ACC, SR1, SR2,
    SS, RS, LS,
):
    f32, bf16 = jnp.float32, jnp.bfloat16
    r, c = lax.axis_index("row"), lax.axis_index("col")
    z, k = r // 2, r % 2
    y, x = c // 4, c % 4
    b = y // 2
    a = (y + b) % 2
    L, TM, CM, G = (LE, LO), (TME, TMO), (CME, CMO), (GE, GO)

    def dev(dx=0, da=0, dk=0, dz=0, db=0):
        xx, zz, kk = (x + dx) % 4, (z + dz) % 4, (k + dk) % 2
        aa, bb = (a + da) % 2, (b + db) % 2
        yy = aa + bb * (3 - 2 * aa)
        return (zz * 2 + kk, yy * 4 + xx)

    def chan(n, src, dst, to):
        return pltpu.make_async_remote_copy(
            src_ref=src, dst_ref=dst, send_sem=SS.at[n], recv_sem=RS.at[n],
            device_id=to, device_id_type=MESH,
        )

    row_peers = [(dx, da, dk) for dk in (0, 1) for da in (0, 1) for dx in range(4) if (dx, da, dk) != (0, 0, 0)]
    col_peers = [(dz, db) for db in (0, 1) for dz in range(4) if (dz, db) != (0, 0)]

    load_i = pltpu.make_async_copy(img_hbm, LE.at[0:B, 0:E], LS.at[0])
    load_t = pltpu.make_async_copy(txt_hbm, LO.at[0:B, 0:E], LS.at[1])
    load_i.start()
    load_t.start()

    barrier = pltpu.get_barrier_semaphore()
    near = [dev(dx=1), dev(dx=3), dev(da=1), dev(dz=1), dev(dz=3), dev(db=1), dev(dk=1)]
    for to in near:
        pl.semaphore_signal(barrier, inc=1, device_id=to, device_id_type=MESH)

    scale = scale_ref[0]
    c2 = scale * LOG2E
    load_i.wait()
    I[0:B, :] = LE[0:B, 0:E].astype(bf16)
    load_t.wait()
    T[0:B, :] = LO[0:B, 0:E].astype(bf16)
    pl.semaphore_wait(barrier, len(near))

    def gather(base, buf, step, slots, plus, minus, partner):
        def at(place, h):
            lo = slots.index(place) * step * B + h * H
            return buf.at[lo : lo + H]

        plan = [
            ("own", (0, 0), partner, (0, 1), (0, 1)),
            ("own", (0, 0), plus, (3, 0), (0, 1)),
            ("own", (0, 0), minus, (1, 0), (1, 0)),
            ("pair", (0, 1), plus, (3, 1), (0,)),
            ("pair", (0, 1), minus, (1, 1), (1,)),
            ("over", (3, 0), partner, (3, 1), (1,)),
            ("over", (1, 0), partner, (1, 1), (0,)),
            ("on", (3, 0), plus, (2, 0), (0,)),
            ("on", (1, 0), minus, (2, 0), (1,)),
            ("on", (3, 1), plus, (2, 1), (0,)),
            ("on", (1, 1), minus, (2, 1), (1,)),
        ]
        out, n = {}, base
        for _, src, to, dst, halves in plan:
            for h in halves:
                out[dst, h, src] = chan(n, at(src, h), at(dst, h), to)
                n += 1
        return out

    xp, xm, pa = dev(dx=1), dev(dx=3), dev(da=1)
    zp, zm, pb = dev(dz=1), dev(dz=3), dev(db=1)
    sib = dev(dk=1)
    gi = gather(GI, I, 2, IMG, xp, xm, pa)
    gt = gather(GT, T, 1, TXT, zp, zm, pb)
    sb = {
        p: chan(SIB + s, I.at[2 * s * B : (2 * s + 1) * B], I.at[(2 * s + 1) * B : (2 * s + 2) * B], sib)
        for s, p in enumerate(IMG)
    }

    def come(cps, dst, h):
        for (to, half, _), cp in cps.items():
            if (to, half) == (dst, h):
                cp.wait_recv()

    for first in (True, False):
        for dst, hh in (((0, 1), (0, 1)), ((3, 0), (0, 1)), ((1, 0), (1, 0))):
            h = hh[0] if first else hh[1]
            gi[dst, h, (0, 0)].start()
            gt[dst, h, (0, 0)].start()
    sb[0, 0].start()
    MC[...] = jnp.full(MC.shape, -1e30, f32)
    SC[...] = jnp.zeros(SC.shape, f32)
    MS[:, :, 0:B] = jnp.full((8, B, B), -1e30, f32)
    MS[:, :, B : 2 * B] = jnp.zeros((8, B, B), f32)
    ACC[...] = jnp.zeros(ACC.shape, f32)

    def images(i):
        return I[pl.ds(pl.multiple_of(i * 2 * B, 2 * B), 2 * B), :]

    def logit_tile(i, jp, e):
        rows = pl.ds(pl.multiple_of(jp * 2 * B + e * B, B), B)
        return c2 * lax.dot_general(images(i), T[rows, :], NT, preferred_element_type=f32)

    def turn(*slots):
        for s in slots:
            GE[0:E, s * B : (s + 1) * B] = T[s * B : (s + 1) * B, :].T

    def lrow(i):
        return pl.multiple_of(jnp.minimum(i, KEPT - 1) * 2 * B, 2 * B)

    def mm_section(i, jp, e):
        cols = pl.ds(pl.multiple_of(jp * 2 * B + e * B, B), B)
        xt = c2 * jnp.dot(images(i), GE[0:E, cols], preferred_element_type=f32)
        L[e][pl.ds(lrow(i), 2 * B), pl.ds(pl.multiple_of(jp * B, B), B)] = xt
        TM[e][...] = jnp.maximum(xt[:, :128], xt[:, 128:])
        CM[e][...] = jnp.max(xt.reshape(2 * B // 8, 8, B), axis=0)

    def st_section(i, jp, e):
        cols = pl.ds(pl.multiple_of(jp * 2 * B + e * B, B), B)
        old = MC[:, cols]
        mc = jnp.maximum(old, CM[e][...])
        MC[:, cols] = mc
        acc = SC[:, cols] * jnp.exp2(old - mc)
        U = 64
        for q in (0, 1):
            for u in range(B // U):
                l = L[e][pl.ds(lrow(i) + q * B + u * U, U), pl.ds(pl.multiple_of(jp * B, B), B)]
                rows, mcol, scol = slice(u * U, (u + 1) * U), slice(q * 128, (q + 1) * 128), slice(B + q * 128, B + (q + 1) * 128)
                old = MS[i, rows, mcol]
                m = jnp.maximum(old, TM[e][q * B + u * U : q * B + (u + 1) * U])
                MS[i, rows, mcol] = m
                MS[i, rows, scol] = (
                    MS[i, rows, scol] * jnp.exp2(old - m) + jnp.exp2(l[:, :128] - m) + jnp.exp2(l[:, 128:] - m)
                )
                acc = acc + jnp.sum(jnp.exp2(l.reshape(U // 8, 8, B) - mc[None]), axis=0)
        SC[:, cols] = acc

    for cps in (gi, gt):
        come(cps, (0, 1), 0)
        cps[(3, 1), 0, (0, 1)].start()
        come(cps, (3, 0), 0)
        cps[(2, 0), 0, (3, 0)].start()
        come(cps, (1, 0), 1)
        cps[(2, 0), 1, (1, 0)].start()
    for cps in (gi, gt):
        come(cps, (0, 1), 1)
        cps[(1, 1), 1, (0, 1)].start()
        come(cps, (3, 0), 1)
        cps[(3, 1), 1, (3, 0)].start()
        come(cps, (1, 0), 0)
        cps[(1, 1), 0, (1, 0)].start()
    sb[0, 1].start()
    sb[3, 0].start()
    sb[1, 0].start()
    for p in ((0, 0), (0, 1), (3, 0), (1, 0)):
        sb[p].wait_recv()

    zero = jnp.int32(0)

    def second():
        for cps in (gi, gt):
            come(cps, (3, 1), 0)
            cps[(2, 1), 0, (3, 1)].start()
            come(cps, (1, 1), 1)
            cps[(2, 1), 1, (1, 1)].start()
        for cps in (gi, gt):
            come(cps, (3, 1), 1)
            come(cps, (1, 1), 0)
        sb[3, 1].start()
        sb[1, 1].start()
        turn(4, 5)

    def fifth():
        sb[3, 1].wait_recv()
        sb[1, 1].wait_recv()

    def eighth():
        for p in ((2, 0), (2, 1)):
            for h in (0, 1):
                come(gi, p, h)
            sb[p].start()
        sb[2, 0].wait_recv()
        sb[2, 1].wait_recv()

    def eleventh():
        for p in ((2, 0), (2, 1)):
            for h in (0, 1):
                come(gt, p, h)
        turn(6, 7)

    def unit(t, carry):
        for n, f in ((3, second), (5, fifth), (8, eighth), (11, eleventh)):
            pl.when(t == n)(f)
        i1, i2, jp = (look_up(t, v) for v in UNITS)
        n1, _, njp = (look_up(t + 1, v) for v in UNITS)
        st_section(i1, jp, 0)
        mm_section(i1, jp, 1)
        st_section(i1, jp, 1)
        mm_section(i2, jp, 0)
        st_section(i2, jp, 0)
        mm_section(i2, jp, 1)
        st_section(i2, jp, 1)
        mm_section(n1, njp, 0)
        return carry

    turn(0, 1, 2, 3)
    mm_section(zero, zero, 0)
    lax.fori_loop(0, 16, unit, 0)

    eye = lax.broadcasted_iota(jnp.int32, (128, 128), 0) == lax.broadcasted_iota(jnp.int32, (128, 128), 1)

    def image_block(i, q):
        return ((k + q) % 2) * 8 + ((a + slot_pair(i, IMG)) % 2) * 4 + (x + slot_ring(i, IMG)) % 4

    def text_block(j):
        return ((b + slot_pair(j, TXT)) % 2) * 4 + (z + slot_ring(j, TXT)) % 4

    def row_lse(i, carry):
        for q in (0, 1):
            m = MS[i, :, q * 128 : (q + 1) * 128]
            s = MS[i, :, B + q * 128 : B + (q + 1) * 128]
            mr = jnp.max(m, axis=1, keepdims=True)
            lse = mr + jnp.log2(jnp.sum(s * jnp.exp2(m - mr), axis=1, keepdims=True))
            for h in (0, 1):
                v = jnp.broadcast_to(lse[h * 128 : (h + 1) * 128], (128, 128))
                RSEND[pl.ds(image_block(i, q) * 2 + h, 1), :] = jnp.sum(jnp.where(eye, v, 0.0), axis=0, keepdims=True)
        return carry

    lax.fori_loop(0, 8, row_lse, 0)
    rows_out = []
    for dx, da, dk in row_peers:
        to, here = dk * 8 + da * 4 + dx, dk * 8 + da * 4 + (4 - dx) % 4
        rows_out.append(chan(ROWS + here, RSEND, RRECV.at[here], dev(dx=dx, da=da, dk=dk)))
        rows_out[-1].start()
    mc = MC[...]
    mr = jnp.max(mc, axis=0, keepdims=True)
    lse = mr + jnp.log2(jnp.sum(SC[...] * jnp.exp2(mc - mr), axis=0, keepdims=True))
    for j in range(8):
        for h in (0, 1):
            CSEND[pl.ds(text_block(jnp.int32(j)) * 2 + h, 1), :] = lse[:, j * B + h * 128 : j * B + (h + 1) * 128]
    cols_out = []
    for dz, db in col_peers:
        here = db * 4 + (4 - dz) % 4
        cols_out.append(chan(COLS + here, CSEND, CRECV.at[here], dev(dz=dz, db=db)))
        cols_out[-1].start()

    for cp in cols_out:
        cp.wait_recv()
    parts = [CSEND[...]] + [CRECV[n] for n in range(1, 8)]
    m = functools.reduce(jnp.maximum, parts)
    CLSE[...] = m + 1.0 + jnp.log2(sum(jnp.exp2(v - m) for v in parts))
    for j in range(8):
        for h in (0, 1):
            MC[:, j * B + h * 128 : j * B + (h + 1) * 128] = jnp.broadcast_to(
                CLSE[pl.ds(text_block(jnp.int32(j)) * 2 + h, 1), :], (8, 128)
            )
    for cp in rows_out:
        cp.wait_recv()
    parts = [RSEND[...]] + [RRECV[n] for n in range(1, 16)]
    m = functools.reduce(jnp.maximum, parts)
    RLSE[...] = m + 1.0 + jnp.log2(sum(jnp.exp2(v - m) for v in parts))

    for cp in [*gi.values(), *gt.values(), *sb.values()]:
        cp.wait_send()

    def spread_rows(i, e):
        for q in (0, 1):
            for h in (0, 1):
                v = RLSE[pl.ds(image_block(i, q) * 2 + h, 1), :]
                v = jnp.sum(jnp.where(eye, jnp.broadcast_to(v, (128, 128)), 0.0), axis=1, keepdims=True)
                TM[e][q * B + h * 128 : q * B + (h + 1) * 128] = jnp.broadcast_to(v, (128, 128))

    def grow(i):
        return pl.multiple_of((i // 2) * 2 * B, 2 * B)

    def grads(i, e):
        U = 32
        acc = ACC[...]
        for q in (0, 1):
            for h in (0, 1):
                rl = TM[e][q * B + h * 128 : q * B + (h + 1) * 128]
                for u in range(128 // U):
                    off = q * B + h * 128 + u * U
                    rb = rl[u * U : (u + 1) * U]
                    rb = jnp.concatenate([rb, rb], axis=1)
                    for j in range(8):
                        l = L[j % 2][pl.ds(lrow(i) + off, U), (j // 2) * B : (j // 2 + 1) * B]
                        cl = MC[:, j * B : (j + 1) * B]
                        g = jnp.exp2(l - rb) + jnp.exp2(l.reshape(U // 8, 8, B) - cl[None]).reshape(U, B)
                        w = jnp.sum((g * l).reshape(U // 8, 8, B), axis=0)
                        acc = acc + w[:, :128] + w[:, 128:]
                        G[e][pl.ds(grow(i) + off, U), j * B : (j + 1) * B] = g.astype(bf16)
        ACC[...] = acc

    def matched(i, par):
        ai, xi = (a + slot_pair(i, IMG)) % 2, (x + slot_ring(i, IMG)) % 4
        yi = ai + b * (3 - 2 * ai)
        here = (x % 2 == b) & ((z + z // 2) % 2 == a) & (xi % 2 == k)
        j = text_slot((2 * (yi % 2) + xi // 2 - z + 4) % 4, (z // 2 + b) % 2)
        for q in (0, 1):
            for e in (0, 1):

                @pl.when(here & ((k + q) % 2 == x // 2) & (j % 2 == e))
                def _():
                    for h in (0, 1):
                        rows = q * B + h * 128
                        l = L[e][pl.ds(lrow(i) + rows, 128), pl.ds(pl.multiple_of((j // 2) * B + h * 128, 128), 128)]
                        cl = MC[0:1, pl.ds(pl.multiple_of(j * B + h * 128, 128), 128)]
                        g = jnp.exp2(l - TM[par][rows : rows + 128]) + jnp.exp2(l - cl)
                        g = jnp.where(eye, g - 1.0, g)
                        G[par][
                            pl.ds(grow(i) + rows, 128),
                            pl.ds(pl.multiple_of(j * B + h * 128, 128), 128),
                        ] = g.astype(bf16)
                        w = jnp.where(eye, l, 0.0)
                        ACC[...] -= jnp.sum(w.reshape(16, 8, 128), axis=0)

    def image_product(i, e):
        p = jnp.dot(G[e][pl.ds(grow(i), 2 * B), :], T[...], preferred_element_type=f32)
        PB[e, 0] = p[:B]
        PB[e, 1] = p[B:]

    def scatter(base, src, own, own_half, fr, xr, ar, ar_half, plus, minus, partner):
        out = {}
        for n, p in enumerate((1, 0)):
            s, lo, hi = base + 6 * n, slice(0, H), slice(H, B)
            out[2, p, 0] = chan(s + 0, src((2, p)).at[lo], fr.at[p, 0], plus)
            out[2, p, 1] = chan(s + 1, src((2, p)).at[hi], fr.at[p, 1], minus)
            out[1, p, 0] = chan(s + 2, src((1, p)).at[lo], xr.at[0, p, lo], plus)
            out[1, p, 1] = chan(s + 3, src((1, p)).at[hi], xr.at[0, p, hi], plus)
            out[3, p, 0] = chan(s + 4, src((3, p)).at[lo], xr.at[1, p, lo], minus)
            out[3, p, 1] = chan(s + 5, src((3, p)).at[hi], xr.at[1, p, hi], minus)
        out[0, 1, 0] = chan(base + 12, own.at[:, 0:W], ar, partner)
        out[0, 1, 1] = chan(base + 13, own_half, ar_half, partner)
        return out

    stage = {(2, 1): 0, (3, 1): 1, (1, 1): 2, (2, 0): 0, (3, 0): 1, (1, 0): 2}
    xs = lambda place: XS.at[stage[place]]
    ts = lambda place: TS.at[stage[place]]
    ltext = lambda s: LE.at[s * B : (s + 1) * B, 0:E]
    ri = scatter(RI, xs, MS.at[1], PS, FR, XR, AR, ARH, xp, xm, pa)
    rt = scatter(RT, ts, ltext(1), PST, FRT, XRT, ART, ARHT, zp, zm, pb)

    def across(i, e):
        return chan(DD + i, PB.at[e, 1], MS.at[i], sib)

    def half(h):
        return pl.ds(h * H, H)

    def free(cps, place):
        if place[1] == 0:
            for h in (0, 1):
                cps[place[0], 1, h].wait_send()

    def send_far(cps, place, p, stage_ref):
        free(cps, place)
        stage_ref[...] = p[...].astype(bf16)
        cps[(*place, 0)].start()
        cps[(*place, 1)].start()

    mixed = {1: 0, 3: 1}

    def send_pure(cps, place, p, stage_ref):
        h = 1 - mixed[place[0]]
        free(cps, place)
        stage_ref[half(h)] = p[half(h)].astype(bf16)
        cps[(*place, h)].start()

    def send_mixed(cps, place, p, stage_ref, fr):
        h = mixed[place[0]]
        cps[2, place[1], h].wait_recv()
        stage_ref[half(h)] = (p[half(h)] + fr[place[1], h].astype(f32)).astype(bf16)
        cps[(*place, h)].start()

    def arrived(cps, pair):
        for ring in (1, 3):
            for h in (0, 1):
                cps[ring, pair, h].wait_recv()

    def send_pair(cps, p, half_ref, xr):
        arrived(cps, 1)
        p[...] += xr[0, 1].astype(f32) + xr[1, 1].astype(f32)
        half_ref[...] = p[:, W:E].astype(bf16)
        cps[0, 1, 0].start()
        cps[0, 1, 1].start()

    def image_sum(s):
        place = IMG[s]
        across(s, s % 2).wait_recv()
        MS[s] += PB[s % 2, 0]
        if place[0] == 2:
            send_far(ri, place, MS.at[s], xs(place))
        elif place[0] % 2:
            send_pure(ri, place, MS.at[s], xs(place))
        across(s, s % 2).wait_send()

    def image_mixed(place):
        send_mixed(ri, place, MS.at[IMG.index(place)], xs(place), FR)

    def again(i):
        @pl.when((i >= KEPT - 1) & (i < 7))
        def _():
            for e in (0, 1):
                for jp in range(4):
                    L[e][(KEPT - 1) * 2 * B : KEPT * 2 * B, jp * B : (jp + 1) * B] = logit_tile(i, jp, e)

    def g_half(i, e):
        again(i)
        grads(i, e)
        image_product(i + 1, 1 - e)
        spread_rows(jnp.maximum(i - 1, 0), 1 - e)
        matched(i, e)
        across(i + 1, 1 - e).start()
        for s in range(7, 1, -1):
            if s % 2 == e:

                @pl.when(i + 2 == s)
                def _():
                    image_sum(s)

    def g_step(t, carry):
        g_half(6 - 2 * t, 0)

        @pl.when(t == 2)
        def _():
            image_mixed((3, 1))
            image_mixed((1, 1))

        g_half(5 - 2 * t, 1)
        return carry

    seven = jnp.int32(7)
    spread_rows(seven, 1)
    grads(seven, 1)
    spread_rows(seven - 1, 0)
    matched(seven, 1)
    lax.fori_loop(0, 3, g_step, 0)
    g_half(zero, 0)

    sc1_out = []
    mine = image_block(zero, 0)
    SR1[mine] = ACC[...]
    for dx, da, dk in row_peers:
        here = dk * 8 + da * 4 + (4 - dx) % 4
        sc1_out.append(chan(SC1 + here, ACC, SR1.at[mine], dev(dx=dx, da=da, dk=dk)))
        sc1_out[-1].start()

    mine_t = text_block(zero)
    sc2_out = [
        chan(SC2 + db * 4 + (4 - dz) % 4, ACC, SR2.at[mine_t], dev(dz=dz, db=db)) for dz, db in col_peers
    ]

    def text_send(kind, place, *more):
        kind(rt, place, ltext(TXT.index(place)), ts(place), *more)

    def text_step(t, carry):
        j = look_up(t, TEXT_ORDER)
        cols = pl.ds(pl.multiple_of(j * B, B), B)
        p = None
        for s in range(8):
            v = lax.dot_general(
                G[s % 2][(s // 2) * 2 * B : (s // 2 + 1) * 2 * B, cols],
                I[s * 2 * B : (s + 1) * 2 * B, :],
                TN, preferred_element_type=f32,
            )
            p = v if p is None else p + v
        LE[pl.ds(pl.multiple_of(j * B, B), B), 0:E] = p

        @pl.when(t == 0)
        def _():
            text_send(send_far, (2, 1))

        @pl.when(t == 1)
        def _():
            text_send(send_pure, (3, 1))
            image_sum(1)

        @pl.when(t == 2)
        def _():
            text_send(send_pure, (1, 1))
            image_mixed((3, 0))
            image_mixed((1, 0))

        @pl.when(t == 3)
        def _():
            text_send(send_mixed, (3, 1), FRT)
            text_send(send_mixed, (1, 1), FRT)
            text_send(send_far, (2, 0))
            send_pair(ri, MS.at[1], PS, XR)

        @pl.when(t == 4)
        def _():
            text_send(send_pure, (3, 0))
            image_product(zero, 0)
            across(zero, 0).start()

        @pl.when(t == 5)
        def _():
            text_send(send_pure, (1, 0))
            for cp in sc1_out:
                cp.wait()
            ACC[...] = sum(SR1[n] for n in range(16))
            SR2[mine_t] = ACC[...]
            for cp in sc2_out:
                cp.start()

        @pl.when(t == 6)
        def _():
            image_sum(0)

        @pl.when(t == 7)
        def _():
            send_pair(rt, ltext(1), PST, XRT)
            text_send(send_mixed, (3, 0), FRT)
            text_send(send_mixed, (1, 0), FRT)

        return carry

    lax.fori_loop(0, 8, text_step, 0)

    def finish(cps, p, xr, ar, ar_half, out, sem):
        arrived(cps, 0)
        p[...] += xr[0, 0].astype(f32) + xr[1, 0].astype(f32)
        cps[0, 1, 0].wait_recv()
        cps[0, 1, 1].wait_recv()
        p[:, 0:W] = scale * (p[:, 0:W] + ar[...])
        p[:, W:E] = scale * (p[:, W:E] + ar_half[...].astype(f32))
        store = pltpu.make_async_copy(p, out, sem)
        store.start()
        return store

    for cp in sc2_out:
        cp.wait()
    gs_ref[0, 0] = jnp.sum(sum(SR2[n] for n in range(8))) / c2
    store_i = finish(ri, MS.at[0], XR, AR, ARH, gi_hbm, LS.at[0])
    store_t = finish(rt, ltext(0), XRT, ART, ARHT, gt_hbm, LS.at[1])

    for cp in rows_out + cols_out:
        cp.wait_send()
    for cps in (ri, rt):
        for (ring, pair, _), cp in cps.items():
            if ring == 0 or pair == 0:
                cp.wait_send()
    store_i.wait()
    store_t.wait()


def on_device(image_embeds, text_embeds, logit_scale):
    f32, bf16 = jnp.float32, jnp.bfloat16
    any_space = pl.BlockSpec(memory_space=pl.ANY)
    smem = pl.BlockSpec(memory_space=pltpu.SMEM)
    grad_image, grad_text, grad_scale = pl.pallas_call(
        kernel,
        out_shape=(
            jax.ShapeDtypeStruct((B, E), f32),
            jax.ShapeDtypeStruct((B, E), f32),
            jax.ShapeDtypeStruct((1, 1), f32),
        ),
        in_specs=[smem, any_space, any_space],
        out_specs=(any_space, any_space, smem),
        scratch_shapes=[
            pltpu.VMEM((16 * B, E), bf16),
            pltpu.VMEM((8 * B, E), bf16),
            pltpu.VMEM((KEPT * 2 * B, 4 * B), f32),
            pltpu.VMEM((KEPT * 2 * B, 4 * B), f32),
            pltpu.VMEM((2 * B, 128), f32),
            pltpu.VMEM((2 * B, 128), f32),
            pltpu.VMEM((8, B), f32),
            pltpu.VMEM((8, B), f32),
            pltpu.VMEM((8 * B, 8 * B), bf16),
            pltpu.VMEM((8 * B, 8 * B), bf16),
            pltpu.VMEM((8, B, E), f32),
            pltpu.VMEM((2, 2, B, E), f32),
            pltpu.VMEM((3, B, E), bf16),
            pltpu.VMEM((3, B, E), bf16),
            pltpu.VMEM((B, E - W), bf16),
            pltpu.VMEM((B, E - W), bf16),
            pltpu.VMEM((2, 2, H, E), bf16),
            pltpu.VMEM((2, 2, B, E), bf16),
            pltpu.VMEM((B, W), f32),
            pltpu.VMEM((B, E - W), bf16),
            pltpu.VMEM((2, 2, H, E), bf16),
            pltpu.VMEM((2, 2, B, E), bf16),
            pltpu.VMEM((B, W), f32),
            pltpu.VMEM((B, E - W), bf16),
            pltpu.VMEM((8, 8 * B), f32),
            pltpu.VMEM((8, 8 * B), f32),
            pltpu.VMEM((32, 128), f32),
            pltpu.VMEM((16, 32, 128), f32),
            pltpu.VMEM((16, 128), f32),
            pltpu.VMEM((8, 16, 128), f32),
            pltpu.VMEM((32, 128), f32),
            pltpu.VMEM((16, 128), f32),
            pltpu.VMEM((8, 128), f32),
            pltpu.VMEM((16, 8, 128), f32),
            pltpu.VMEM((8, 8, 128), f32),
            pltpu.SemaphoreType.DMA((CHANNELS,)),
            pltpu.SemaphoreType.DMA((CHANNELS,)),
            pltpu.SemaphoreType.DMA((2,)),
        ],
        compiler_params=pltpu.CompilerParams(
            collective_id=0, has_side_effects=True, vmem_limit_bytes=64 << 20
        ),
        cost_estimate=pl.CostEstimate(flops=6 * 4096 * 2048 * 512, bytes_accessed=4 << 20, transcendentals=4 * 4096 * 2048),
    )(logit_scale.reshape(1), image_embeds, text_embeds)
    return grad_image, grad_text, grad_scale.reshape(())


def solution(mesh):
    return jax.shard_map(
        on_device,
        mesh=mesh,
        in_specs=(P(("row", "col"), None), P(("col", "row"), None), P()),
        out_specs=(P(("row", "col"), None), P(("col", "row"), None), P()),
        check_vma=False,
    )
```

```python
import functools

import jax
import jax.numpy as jnp
from jax import lax
from jax.experimental import pallas as pl
from jax.experimental.pallas import tpu as pltpu
from jax.sharding import PartitionSpec as P

MESH = pl.DeviceIdType.MESH
NT = (((1,), (1,)), ((), ()))
TN = (((0,), (0,)), ((), ()))
LOG2E = 1.4426950408889634
B = 256
E = 512
H = B // 2
W = E // 2
KEPT = 2

IMG = ((0, 0), (0, 1), (1, 0), (3, 0), (2, 0), (1, 1), (3, 1), (2, 1))
TXT = ((0, 0), (0, 1), (1, 0), (3, 0), (1, 1), (3, 1), (2, 0), (2, 1))
TEXT_ORDER = (7, 5, 4, 6, 3, 2, 1, 0)
EVEN, ODD = (0, 2, 6, 4), (1, 3, 5, 7)

GI, GT, SIB, RI, RT, DD = 0, 14, 28, 36, 50, 64
ROWS, COLS, SC1, SC2, CHANNELS = 72, 88, 96, 112, 120


def look_up(i, values):
    return sum(v * (i == n).astype(jnp.int32) for n, v in enumerate(values) if v)


def slot_ring(i, slots):
    return look_up(i, [d for d, _ in slots])


def slot_pair(i, slots):
    return look_up(i, [d for _, d in slots])


def text_slot(ring, pair):
    return sum(
        s * ((ring == d) & (pair == e)).astype(jnp.int32)
        for s, (d, e) in enumerate(TXT)
        if s
    )


def kernel(
    scale_ref, img_hbm, txt_hbm, gi_hbm, gt_hbm, gs_ref,
    I, T, LE, LO, TME, TMO, CME, CMO, GE, GO, MS, PB, XS, TS, PS, PST, FR, XR, AR, ARH, FRT, XRT, ART, ARHT,
    MC, SC, RSEND, RRECV, CSEND, CRECV, RLSE, CLSE, ACC, SR1, SR2,
    SS, RS, LS,
):
    f32, bf16 = jnp.float32, jnp.bfloat16
    r, c = lax.axis_index("row"), lax.axis_index("col")
    z, k = r // 2, r % 2
    y, x = c // 4, c % 4
    b = y // 2
    a = (y + b) % 2
    L, TM, CM, G = (LE, LO), (TME, TMO), (CME, CMO), (GE, GO)

    def dev(dx=0, da=0, dk=0, dz=0, db=0):
        xx, zz, kk = (x + dx) % 4, (z + dz) % 4, (k + dk) % 2
        aa, bb = (a + da) % 2, (b + db) % 2
        yy = aa + bb * (3 - 2 * aa)
        return (zz * 2 + kk, yy * 4 + xx)

    def chan(n, src, dst, to):
        return pltpu.make_async_remote_copy(
            src_ref=src, dst_ref=dst, send_sem=SS.at[n], recv_sem=RS.at[n],
            device_id=to, device_id_type=MESH,
        )

    row_peers = [(dx, da, dk) for dk in (0, 1) for da in (0, 1) for dx in range(4) if (dx, da, dk) != (0, 0, 0)]
    col_peers = [(dz, db) for db in (0, 1) for dz in range(4) if (dz, db) != (0, 0)]

    load_i = pltpu.make_async_copy(img_hbm, LE.at[0:B, 0:E], LS.at[0])
    load_t = pltpu.make_async_copy(txt_hbm, LO.at[0:B, 0:E], LS.at[1])
    load_i.start()
    load_t.start()

    barrier = pltpu.get_barrier_semaphore()
    near = [dev(dx=1), dev(dx=3), dev(da=1), dev(dz=1), dev(dz=3), dev(db=1), dev(dk=1)]
    for to in near:
        pl.semaphore_signal(barrier, inc=1, device_id=to, device_id_type=MESH)

    scale = scale_ref[0]
    c2 = scale * LOG2E
    load_i.wait()
    I[0:B, :] = LE[0:B, 0:E].astype(bf16)
    load_t.wait()
    T[0:B, :] = LO[0:B, 0:E].astype(bf16)
    pl.semaphore_wait(barrier, len(near))

    def gather(base, buf, step, slots, plus, minus, partner):
        def at(place, h):
            lo = slots.index(place) * step * B + h * H
            return buf.at[lo : lo + H]

        plan = [
            ("own", (0, 0), partner, (0, 1), (0, 1)),
            ("own", (0, 0), plus, (3, 0), (0, 1)),
            ("own", (0, 0), minus, (1, 0), (1, 0)),
            ("pair", (0, 1), plus, (3, 1), (0,)),
            ("pair", (0, 1), minus, (1, 1), (1,)),
            ("over", (3, 0), partner, (3, 1), (1,)),
            ("over", (1, 0), partner, (1, 1), (0,)),
            ("on", (3, 0), plus, (2, 0), (0,)),
            ("on", (1, 0), minus, (2, 0), (1,)),
            ("on", (3, 1), plus, (2, 1), (0,)),
            ("on", (1, 1), minus, (2, 1), (1,)),
        ]
        out, n = {}, base
        for _, src, to, dst, halves in plan:
            for h in halves:
                out[dst, h, src] = chan(n, at(src, h), at(dst, h), to)
                n += 1
        return out

    xp, xm, pa = dev(dx=1), dev(dx=3), dev(da=1)
    zp, zm, pb = dev(dz=1), dev(dz=3), dev(db=1)
    sib = dev(dk=1)
    gi = gather(GI, I, 2, IMG, xp, xm, pa)
    gt = gather(GT, T, 1, TXT, zp, zm, pb)
    sb = {
        p: chan(SIB + s, I.at[2 * s * B : (2 * s + 1) * B], I.at[(2 * s + 1) * B : (2 * s + 2) * B], sib)
        for s, p in enumerate(IMG)
    }

    def come(cps, dst, h):
        for (to, half, _), cp in cps.items():
            if (to, half) == (dst, h):
                cp.wait_recv()

    for first in (True, False):
        for dst, hh in (((0, 1), (0, 1)), ((3, 0), (0, 1)), ((1, 0), (1, 0))):
            h = hh[0] if first else hh[1]
            gi[dst, h, (0, 0)].start()
            gt[dst, h, (0, 0)].start()
    sb[0, 0].start()
    MC[...] = jnp.full(MC.shape, -1e30, f32)
    SC[...] = jnp.zeros(SC.shape, f32)
    MS[:, :, 0:B] = jnp.full((8, B, B), -1e30, f32)
    MS[:, :, B : 2 * B] = jnp.zeros((8, B, B), f32)
    ACC[...] = jnp.zeros(ACC.shape, f32)

    def images(i):
        return I[pl.ds(pl.multiple_of(i * 2 * B, 2 * B), 2 * B), :]

    def images(i):
        return I[pl.ds(pl.multiple_of(i * 2 * B, 2 * B), 2 * B), :]

    def logit_tile(i, j):
        return c2 * lax.dot_general(images(i), T[j * B : (j + 1) * B, :], NT, preferred_element_type=f32)

    def lrow(i, e):
        return pl.multiple_of((jnp.minimum(i // 2, KEPT - 1) if e else i // 2) * 2 * B, 2 * B)

    def mm_section(i, jp, e):
        for n in (0, 1):
            j = 2 * jp + n
            xt = logit_tile(i, j)
            L[e][pl.ds(lrow(i, e), 2 * B), j * B : (j + 1) * B] = xt
            top = jnp.maximum(xt[:, :128], xt[:, 128:])
            TM[e][...] = jnp.maximum(TM[e][...], top) if n else top
            CM[e][:, n * B : (n + 1) * B] = jnp.max(xt.reshape(2 * B // 8, 8, B), axis=0)

    def st_section(i, jp, e):
        cols = slice(jp * 2 * B, (jp + 1) * 2 * B)
        old = MC[:, cols]
        mc = jnp.maximum(old, CM[e][...])
        MC[:, cols] = mc
        acc = SC[:, cols] * jnp.exp2(old - mc)
        U = 64
        for q in (0, 1):
            for u in range(B // U):
                l = L[e][pl.ds(lrow(i, e) + q * B + u * U, U), cols]
                rows, mcol, scol = slice(u * U, (u + 1) * U), slice(q * 128, (q + 1) * 128), slice(B + q * 128, B + (q + 1) * 128)
                old = MS[i, rows, mcol]
                m = jnp.maximum(old, TM[e][q * B + u * U : q * B + (u + 1) * U])
                MS[i, rows, mcol] = m
                s = MS[i, rows, scol] * jnp.exp2(old - m)
                for v in range(4):
                    s = s + jnp.exp2(l[:, v * 128 : (v + 1) * 128] - m)
                MS[i, rows, scol] = s
                acc = acc + jnp.sum(jnp.exp2(l.reshape(U // 8, 8, 2 * B) - mc[None]), axis=0)
        SC[:, cols] = acc

    for cps in (gi, gt):
        come(cps, (0, 1), 0)
        cps[(3, 1), 0, (0, 1)].start()
        come(cps, (3, 0), 0)
        cps[(2, 0), 0, (3, 0)].start()
        come(cps, (1, 0), 1)
        cps[(2, 0), 1, (1, 0)].start()
    for cps in (gi, gt):
        come(cps, (0, 1), 1)
        cps[(1, 1), 1, (0, 1)].start()
        come(cps, (3, 0), 1)
        cps[(3, 1), 1, (3, 0)].start()
        come(cps, (1, 0), 0)
        cps[(1, 1), 0, (1, 0)].start()
    sb[0, 1].start()
    sb[3, 0].start()
    sb[1, 0].start()
    for p in ((0, 0), (0, 1), (3, 0), (1, 0)):
        sb[p].wait_recv()

    zero = jnp.int32(0)

    def second():
        for cps in (gi, gt):
            come(cps, (3, 1), 0)
            cps[(2, 1), 0, (3, 1)].start()
            come(cps, (1, 1), 1)
            cps[(2, 1), 1, (1, 1)].start()
        for cps in (gi, gt):
            come(cps, (3, 1), 1)
            come(cps, (1, 1), 0)
        sb[3, 1].start()
        sb[1, 1].start()

    def third():
        for p in ((2, 0), (2, 1)):
            for h in (0, 1):
                come(gi, p, h)
            sb[p].start()
        sb[2, 0].wait_recv()
        sb[2, 1].wait_recv()

    def pairs(first, count, jps, ahead, before=None):
        last = first + count - 1

        def one(t, carry):
            if before is not None:
                pl.when(t == last)(before)
            ev, od = look_up(t, EVEN), look_up(t, ODD)
            if not ahead:
                mm_section(ev, jps[0], 0)
            for n, jp in enumerate(jps):
                st_section(ev, jp, 0)
                mm_section(od, jp, 1)
                st_section(od, jp, 1)
                if n + 1 < len(jps):
                    mm_section(ev, jps[n + 1], 0)
                elif ahead:
                    mm_section(look_up(jnp.minimum(t + 1, last), EVEN), jps[0], 0)
            return carry

        if ahead:
            mm_section(jnp.int32(EVEN[first]), jps[0], 0)
        lax.fori_loop(first, first + count, one, 0)

    pairs(0, 2, (0, 1), True)
    second()
    pairs(0, 2, (2,), True)
    sb[3, 1].wait_recv()
    sb[1, 1].wait_recv()
    pairs(2, 2, (0, 1, 2), False, third)
    for p in ((2, 0), (2, 1)):
        for h in (0, 1):
            come(gt, p, h)
    pairs(0, 4, (3,), True)

    eye = lax.broadcasted_iota(jnp.int32, (128, 128), 0) == lax.broadcasted_iota(jnp.int32, (128, 128), 1)

    def image_block(i, q):
        return ((k + q) % 2) * 8 + ((a + slot_pair(i, IMG)) % 2) * 4 + (x + slot_ring(i, IMG)) % 4

    def text_block(j):
        return ((b + slot_pair(j, TXT)) % 2) * 4 + (z + slot_ring(j, TXT)) % 4

    def row_lse(i, carry):
        for q in (0, 1):
            m = MS[i, :, q * 128 : (q + 1) * 128]
            s = MS[i, :, B + q * 128 : B + (q + 1) * 128]
            mr = jnp.max(m, axis=1, keepdims=True)
            lse = mr + jnp.log2(jnp.sum(s * jnp.exp2(m - mr), axis=1, keepdims=True))
            for h in (0, 1):
                v = jnp.broadcast_to(lse[h * 128 : (h + 1) * 128], (128, 128))
                RSEND[pl.ds(image_block(i, q) * 2 + h, 1), :] = jnp.sum(jnp.where(eye, v, 0.0), axis=0, keepdims=True)
        return carry

    lax.fori_loop(0, 8, row_lse, 0)
    rows_out = []
    for dx, da, dk in row_peers:
        to, here = dk * 8 + da * 4 + dx, dk * 8 + da * 4 + (4 - dx) % 4
        rows_out.append(chan(ROWS + here, RSEND, RRECV.at[here], dev(dx=dx, da=da, dk=dk)))
        rows_out[-1].start()
    mc = MC[...]
    mr = jnp.max(mc, axis=0, keepdims=True)
    lse = mr + jnp.log2(jnp.sum(SC[...] * jnp.exp2(mc - mr), axis=0, keepdims=True))
    for j in range(8):
        for h in (0, 1):
            CSEND[pl.ds(text_block(jnp.int32(j)) * 2 + h, 1), :] = lse[:, j * B + h * 128 : j * B + (h + 1) * 128]
    cols_out = []
    for dz, db in col_peers:
        here = db * 4 + (4 - dz) % 4
        cols_out.append(chan(COLS + here, CSEND, CRECV.at[here], dev(dz=dz, db=db)))
        cols_out[-1].start()

    for cp in cols_out:
        cp.wait_recv()
    parts = [CSEND[...]] + [CRECV[n] for n in range(1, 8)]
    m = functools.reduce(jnp.maximum, parts)
    CLSE[...] = m + 1.0 + jnp.log2(sum(jnp.exp2(v - m) for v in parts))
    for j in range(8):
        for h in (0, 1):
            MC[:, j * B + h * 128 : j * B + (h + 1) * 128] = jnp.broadcast_to(
                CLSE[pl.ds(text_block(jnp.int32(j)) * 2 + h, 1), :], (8, 128)
            )
    for cp in rows_out:
        cp.wait_recv()
    parts = [RSEND[...]] + [RRECV[n] for n in range(1, 16)]
    m = functools.reduce(jnp.maximum, parts)
    RLSE[...] = m + 1.0 + jnp.log2(sum(jnp.exp2(v - m) for v in parts))

    for cp in [*gi.values(), *gt.values(), *sb.values()]:
        cp.wait_send()

    def spread_rows(i, e):
        for q in (0, 1):
            for h in (0, 1):
                v = RLSE[pl.ds(image_block(i, q) * 2 + h, 1), :]
                v = jnp.sum(jnp.where(eye, jnp.broadcast_to(v, (128, 128)), 0.0), axis=1, keepdims=True)
                TM[e][q * B + h * 128 : q * B + (h + 1) * 128] = jnp.broadcast_to(v, (128, 128))

    def grow(i):
        return pl.multiple_of((i // 2) * 2 * B, 2 * B)

    def grads(i, e):
        U = 32
        acc = ACC[...]
        for q in (0, 1):
            for h in (0, 1):
                rl = TM[e][q * B + h * 128 : q * B + (h + 1) * 128]
                for u in range(128 // U):
                    off = q * B + h * 128 + u * U
                    rb = rl[u * U : (u + 1) * U]
                    rb = jnp.concatenate([rb, rb], axis=1)
                    for j in range(8):
                        l = L[e][pl.ds(lrow(i, e) + off, U), j * B : (j + 1) * B]
                        cl = MC[:, j * B : (j + 1) * B]
                        g = jnp.exp2(l - rb) + jnp.exp2(l.reshape(U // 8, 8, B) - cl[None]).reshape(U, B)
                        w = jnp.sum((g * l).reshape(U // 8, 8, B), axis=0)
                        acc = acc + w[:, :128] + w[:, 128:]
                        G[e][pl.ds(grow(i) + off, U), j * B : (j + 1) * B] = g.astype(bf16)
        ACC[...] = acc

    def matched(i, par):
        ai, xi = (a + slot_pair(i, IMG)) % 2, (x + slot_ring(i, IMG)) % 4
        yi = ai + b * (3 - 2 * ai)
        here = (x % 2 == b) & ((z + z // 2) % 2 == a) & (xi % 2 == k)
        j = text_slot((2 * (yi % 2) + xi // 2 - z + 4) % 4, (z // 2 + b) % 2)
        for q in (0, 1):

            @pl.when(here & ((k + q) % 2 == x // 2))
            def _():
                for h in (0, 1):
                    rows = q * B + h * 128
                    cols = pl.ds(pl.multiple_of(j * B + h * 128, 128), 128)
                    l = L[par][pl.ds(lrow(i, par) + rows, 128), cols]
                    g = jnp.exp2(l - TM[par][rows : rows + 128]) + jnp.exp2(l - MC[0:1, cols])
                    g = jnp.where(eye, g - 1.0, g)
                    G[par][pl.ds(grow(i) + rows, 128), cols] = g.astype(bf16)
                    w = jnp.where(eye, l, 0.0)
                    ACC[...] -= jnp.sum(w.reshape(16, 8, 128), axis=0)

    def image_product(i, e):
        p = jnp.dot(G[e][pl.ds(grow(i), 2 * B), :], T[...], preferred_element_type=f32)
        PB[e, 0] = p[:B]
        PB[e, 1] = p[B:]

    def scatter(base, src, own, own_half, fr, xr, ar, ar_half, plus, minus, partner):
        out = {}
        for n, p in enumerate((1, 0)):
            s, lo, hi = base + 6 * n, slice(0, H), slice(H, B)
            out[2, p, 0] = chan(s + 0, src((2, p)).at[lo], fr.at[p, 0], plus)
            out[2, p, 1] = chan(s + 1, src((2, p)).at[hi], fr.at[p, 1], minus)
            out[1, p, 0] = chan(s + 2, src((1, p)).at[lo], xr.at[0, p, lo], plus)
            out[1, p, 1] = chan(s + 3, src((1, p)).at[hi], xr.at[0, p, hi], plus)
            out[3, p, 0] = chan(s + 4, src((3, p)).at[lo], xr.at[1, p, lo], minus)
            out[3, p, 1] = chan(s + 5, src((3, p)).at[hi], xr.at[1, p, hi], minus)
        out[0, 1, 0] = chan(base + 12, own.at[:, 0:W], ar, partner)
        out[0, 1, 1] = chan(base + 13, own_half, ar_half, partner)
        return out

    stage = {(2, 1): 0, (3, 1): 1, (1, 1): 2, (2, 0): 0, (3, 0): 1, (1, 0): 2}
    xs = lambda place: XS.at[stage[place]]
    ts = lambda place: TS.at[stage[place]]
    ltext = lambda s: LE.at[s * B : (s + 1) * B, 0:E]
    ri = scatter(RI, xs, MS.at[1], PS, FR, XR, AR, ARH, xp, xm, pa)
    rt = scatter(RT, ts, ltext(1), PST, FRT, XRT, ART, ARHT, zp, zm, pb)

    def across(i, e):
        return chan(DD + i, PB.at[e, 1], MS.at[i], sib)

    def half(h):
        return pl.ds(h * H, H)

    def free(cps, place):
        if place[1] == 0:
            for h in (0, 1):
                cps[place[0], 1, h].wait_send()

    def send_far(cps, place, p, stage_ref):
        free(cps, place)
        stage_ref[...] = p[...].astype(bf16)
        cps[(*place, 0)].start()
        cps[(*place, 1)].start()

    mixed = {1: 0, 3: 1}

    def send_pure(cps, place, p, stage_ref):
        h = 1 - mixed[place[0]]
        free(cps, place)
        stage_ref[half(h)] = p[half(h)].astype(bf16)
        cps[(*place, h)].start()

    def send_mixed(cps, place, p, stage_ref, fr):
        h = mixed[place[0]]
        cps[2, place[1], h].wait_recv()
        stage_ref[half(h)] = (p[half(h)] + fr[place[1], h].astype(f32)).astype(bf16)
        cps[(*place, h)].start()

    def arrived(cps, pair):
        for ring in (1, 3):
            for h in (0, 1):
                cps[ring, pair, h].wait_recv()

    def send_pair(cps, p, half_ref, xr):
        arrived(cps, 1)
        p[...] += xr[0, 1].astype(f32) + xr[1, 1].astype(f32)
        half_ref[...] = p[:, W:E].astype(bf16)
        cps[0, 1, 0].start()
        cps[0, 1, 1].start()

    def image_sum(s):
        place = IMG[s]
        across(s, s % 2).wait_recv()
        MS[s] += PB[s % 2, 0]
        if place[0] == 2:
            send_far(ri, place, MS.at[s], xs(place))
        elif place[0] % 2:
            send_pure(ri, place, MS.at[s], xs(place))
        across(s, s % 2).wait_send()

    def image_mixed(place):
        send_mixed(ri, place, MS.at[IMG.index(place)], xs(place), FR)

    def again(i):
        for j in range(8):
            L[1][(KEPT - 1) * 2 * B : KEPT * 2 * B, j * B : (j + 1) * B] = logit_tile(i, j)

    def g_half(i, e):
        if e:
            pl.when(i >= 2 * KEPT - 1)(lambda: again(i))
        grads(i, e)
        image_product(i + 1, 1 - e)
        spread_rows(jnp.maximum(i - 1, 0), 1 - e)
        matched(i, e)
        across(i + 1, 1 - e).start()
        for s in range(7, 1, -1):
            if s % 2 == e:

                @pl.when(i + 2 == s)
                def _():
                    image_sum(s)

    def g_step(t, carry):
        g_half(6 - 2 * t, 0)

        @pl.when(t == 2)
        def _():
            image_mixed((3, 1))
            image_mixed((1, 1))

        g_half(5 - 2 * t, 1)
        return carry

    seven = jnp.int32(7)
    spread_rows(seven, 1)
    grads(seven, 1)
    spread_rows(seven - 1, 0)
    matched(seven, 1)
    lax.fori_loop(0, 3, g_step, 0)
    g_half(zero, 0)

    sc1_out = []
    mine = image_block(zero, 0)
    SR1[mine] = ACC[...]
    for dx, da, dk in row_peers:
        here = dk * 8 + da * 4 + (4 - dx) % 4
        sc1_out.append(chan(SC1 + here, ACC, SR1.at[mine], dev(dx=dx, da=da, dk=dk)))
        sc1_out[-1].start()

    mine_t = text_block(zero)
    sc2_out = [
        chan(SC2 + db * 4 + (4 - dz) % 4, ACC, SR2.at[mine_t], dev(dz=dz, db=db)) for dz, db in col_peers
    ]

    def text_send(kind, place, *more):
        kind(rt, place, ltext(TXT.index(place)), ts(place), *more)

    def text_step(t, carry):
        j = look_up(t, TEXT_ORDER)
        cols = pl.ds(pl.multiple_of(j * B, B), B)
        p = None
        for s in range(8):
            v = lax.dot_general(
                G[s % 2][(s // 2) * 2 * B : (s // 2 + 1) * 2 * B, cols],
                I[s * 2 * B : (s + 1) * 2 * B, :],
                TN, preferred_element_type=f32,
            )
            p = v if p is None else p + v
        LE[pl.ds(pl.multiple_of(j * B, B), B), 0:E] = p

        @pl.when(t == 0)
        def _():
            text_send(send_far, (2, 1))

        @pl.when(t == 1)
        def _():
            text_send(send_pure, (3, 1))
            image_sum(1)

        @pl.when(t == 2)
        def _():
            text_send(send_pure, (1, 1))
            image_mixed((3, 0))
            image_mixed((1, 0))

        @pl.when(t == 3)
        def _():
            text_send(send_mixed, (3, 1), FRT)
            text_send(send_mixed, (1, 1), FRT)
            text_send(send_far, (2, 0))
            send_pair(ri, MS.at[1], PS, XR)

        @pl.when(t == 4)
        def _():
            text_send(send_pure, (3, 0))
            image_product(zero, 0)
            across(zero, 0).start()

        @pl.when(t == 5)
        def _():
            text_send(send_pure, (1, 0))
            for cp in sc1_out:
                cp.wait()
            ACC[...] = sum(SR1[n] for n in range(16))
            SR2[mine_t] = ACC[...]
            for cp in sc2_out:
                cp.start()

        @pl.when(t == 6)
        def _():
            image_sum(0)

        @pl.when(t == 7)
        def _():
            send_pair(rt, ltext(1), PST, XRT)
            text_send(send_mixed, (3, 0), FRT)
            text_send(send_mixed, (1, 0), FRT)

        return carry

    lax.fori_loop(0, 8, text_step, 0)

    def finish(cps, p, xr, ar, ar_half, out, sem):
        arrived(cps, 0)
        p[...] += xr[0, 0].astype(f32) + xr[1, 0].astype(f32)
        cps[0, 1, 0].wait_recv()
        cps[0, 1, 1].wait_recv()
        p[:, 0:W] = scale * (p[:, 0:W] + ar[...])
        p[:, W:E] = scale * (p[:, W:E] + ar_half[...].astype(f32))
        store = pltpu.make_async_copy(p, out, sem)
        store.start()
        return store

    for cp in sc2_out:
        cp.wait()
    gs_ref[0, 0] = jnp.sum(sum(SR2[n] for n in range(8))) / c2
    store_i = finish(ri, MS.at[0], XR, AR, ARH, gi_hbm, LS.at[0])
    store_t = finish(rt, ltext(0), XRT, ART, ARHT, gt_hbm, LS.at[1])

    for cp in rows_out + cols_out:
        cp.wait_send()
    for cps in (ri, rt):
        for (ring, pair, _), cp in cps.items():
            if ring == 0 or pair == 0:
                cp.wait_send()
    store_i.wait()
    store_t.wait()


def on_device(image_embeds, text_embeds, logit_scale):
    f32, bf16 = jnp.float32, jnp.bfloat16
    any_space = pl.BlockSpec(memory_space=pl.ANY)
    smem = pl.BlockSpec(memory_space=pltpu.SMEM)
    grad_image, grad_text, grad_scale = pl.pallas_call(
        kernel,
        out_shape=(
            jax.ShapeDtypeStruct((B, E), f32),
            jax.ShapeDtypeStruct((B, E), f32),
            jax.ShapeDtypeStruct((1, 1), f32),
        ),
        in_specs=[smem, any_space, any_space],
        out_specs=(any_space, any_space, smem),
        scratch_shapes=[
            pltpu.VMEM((16 * B, E), bf16),
            pltpu.VMEM((8 * B, E), bf16),
            pltpu.VMEM((8 * B, 8 * B), f32),
            pltpu.VMEM((KEPT * 2 * B, 8 * B), f32),
            pltpu.VMEM((2 * B, 128), f32),
            pltpu.VMEM((2 * B, 128), f32),
            pltpu.VMEM((8, 2 * B), f32),
            pltpu.VMEM((8, 2 * B), f32),
            pltpu.VMEM((8 * B, 8 * B), bf16),
            pltpu.VMEM((8 * B, 8 * B), bf16),
            pltpu.VMEM((8, B, E), f32),
            pltpu.VMEM((2, 2, B, E), f32),
            pltpu.VMEM((3, B, E), bf16),
            pltpu.VMEM((3, B, E), bf16),
            pltpu.VMEM((B, E - W), bf16),
            pltpu.VMEM((B, E - W), bf16),
            pltpu.VMEM((2, 2, H, E), bf16),
            pltpu.VMEM((2, 2, B, E), bf16),
            pltpu.VMEM((B, W), f32),
            pltpu.VMEM((B, E - W), bf16),
            pltpu.VMEM((2, 2, H, E), bf16),
            pltpu.VMEM((2, 2, B, E), bf16),
            pltpu.VMEM((B, W), f32),
            pltpu.VMEM((B, E - W), bf16),
            pltpu.VMEM((8, 8 * B), f32),
            pltpu.VMEM((8, 8 * B), f32),
            pltpu.VMEM((32, 128), f32),
            pltpu.VMEM((16, 32, 128), f32),
            pltpu.VMEM((16, 128), f32),
            pltpu.VMEM((8, 16, 128), f32),
            pltpu.VMEM((32, 128), f32),
            pltpu.VMEM((16, 128), f32),
            pltpu.VMEM((8, 128), f32),
            pltpu.VMEM((16, 8, 128), f32),
            pltpu.VMEM((8, 8, 128), f32),
            pltpu.SemaphoreType.DMA((CHANNELS,)),
            pltpu.SemaphoreType.DMA((CHANNELS,)),
            pltpu.SemaphoreType.DMA((2,)),
        ],
        compiler_params=pltpu.CompilerParams(
            collective_id=0, has_side_effects=True, vmem_limit_bytes=64 << 20
        ),
        cost_estimate=pl.CostEstimate(flops=6 * 4096 * 2048 * 512, bytes_accessed=4 << 20, transcendentals=4 * 4096 * 2048),
    )(logit_scale.reshape(1), image_embeds, text_embeds)
    return grad_image, grad_text, grad_scale.reshape(())


def solution(mesh):
    return jax.shard_map(
        on_device,
        mesh=mesh,
        in_specs=(P(("row", "col"), None), P(("col", "row"), None), P()),
        out_specs=(P(("row", "col"), None), P(("col", "row"), None), P()),
        check_vma=False,
    )
```

```python
import functools

import jax
import jax.numpy as jnp
from jax import lax
from jax.experimental import pallas as pl
from jax.experimental.pallas import tpu as pltpu
from jax.sharding import PartitionSpec as P

MESH = pl.DeviceIdType.MESH
NT = (((1,), (1,)), ((), ()))
TN = (((0,), (0,)), ((), ()))
LOG2E = 1.4426950408889634
B = 256
E = 512
H = B // 2
W = E // 2
KEPT = 2

IMG = ((0, 0), (0, 1), (1, 0), (3, 0), (2, 0), (1, 1), (3, 1), (2, 1))
TXT = ((0, 0), (0, 1), (1, 0), (3, 0), (1, 1), (3, 1), (2, 0), (2, 1))
TEXT_ORDER = (7, 5, 4, 6, 3, 2, 1, 0)
EVEN, ODD = (0, 2, 6, 4), (1, 3, 5, 7)

GI, GT, SIB, RI, RT, DD = 0, 14, 28, 36, 50, 64
ROWS, COLS, SC1, SC2, CHANNELS = 72, 88, 96, 112, 120


def look_up(i, values):
    return sum(v * (i == n).astype(jnp.int32) for n, v in enumerate(values) if v)


def slot_ring(i, slots):
    return look_up(i, [d for d, _ in slots])


def slot_pair(i, slots):
    return look_up(i, [d for _, d in slots])


def text_slot(ring, pair):
    return sum(
        s * ((ring == d) & (pair == e)).astype(jnp.int32)
        for s, (d, e) in enumerate(TXT)
        if s
    )


def kernel(
    scale_ref, img_hbm, txt_hbm, out_hbm, gs_ref,
    I, T, LE, LO, TME, TMO, CME, CMO, GE, GO, MS, PB, XS, TS, PS, PST, FR, XR, AR, ARH, FRT, XRT, ART, ARHT,
    MC, SC, RSEND, RRECV, CSEND, CRECV, RLSE, CLSE, ACC, SR1, SR2,
    SS, RS, LS,
):
    f32, bf16 = jnp.float32, jnp.bfloat16
    r, c = lax.axis_index("row"), lax.axis_index("col")
    z, k = r // 2, r % 2
    y, x = c // 4, c % 4
    b = y // 2
    a = (y + b) % 2
    L, TM, CM, G = (LE, LO), (TME, TMO), (CME, CMO), (GE, GO)

    def dev(dx=0, da=0, dk=0, dz=0, db=0):
        xx, zz, kk = (x + dx) % 4, (z + dz) % 4, (k + dk) % 2
        aa, bb = (a + da) % 2, (b + db) % 2
        yy = aa + bb * (3 - 2 * aa)
        return (zz * 2 + kk, yy * 4 + xx)

    def chan(n, src, dst, to):
        return pltpu.make_async_remote_copy(
            src_ref=src, dst_ref=dst, send_sem=SS.at[n], recv_sem=RS.at[n],
            device_id=to, device_id_type=MESH,
        )

    row_peers = [(dx, da, dk) for dk in (0, 1) for da in (0, 1) for dx in range(4) if (dx, da, dk) != (0, 0, 0)]
    col_peers = [(dz, db) for db in (0, 1) for dz in range(4) if (dz, db) != (0, 0)]

    load_i = pltpu.make_async_copy(img_hbm, LE.at[0:B, 0:E], LS.at[0])
    load_t = pltpu.make_async_copy(txt_hbm, LO.at[0:B, 0:E], LS.at[1])
    load_i.start()
    load_t.start()

    barrier = pltpu.get_barrier_semaphore()
    near = [dev(dx=1), dev(dx=3), dev(da=1), dev(dz=1), dev(dz=3), dev(db=1), dev(dk=1)]
    for to in near:
        pl.semaphore_signal(barrier, inc=1, device_id=to, device_id_type=MESH)

    scale = scale_ref[0]
    c2 = scale * LOG2E
    load_i.wait()
    I[0:B, :] = LE[0:B, 0:E].astype(bf16)
    load_t.wait()
    T[0:B, :] = LO[0:B, 0:E].astype(bf16)
    pl.semaphore_wait(barrier, len(near))

    def gather(base, buf, step, slots, plus, minus, partner):
        def at(place, h):
            lo = slots.index(place) * step * B + h * H
            return buf.at[lo : lo + H]

        plan = [
            ("own", (0, 0), partner, (0, 1), (0, 1)),
            ("own", (0, 0), plus, (3, 0), (0, 1)),
            ("own", (0, 0), minus, (1, 0), (1, 0)),
            ("pair", (0, 1), plus, (3, 1), (0,)),
            ("pair", (0, 1), minus, (1, 1), (1,)),
            ("over", (3, 0), partner, (3, 1), (1,)),
            ("over", (1, 0), partner, (1, 1), (0,)),
            ("on", (3, 0), plus, (2, 0), (0,)),
            ("on", (1, 0), minus, (2, 0), (1,)),
            ("on", (3, 1), plus, (2, 1), (0,)),
            ("on", (1, 1), minus, (2, 1), (1,)),
        ]
        out, n = {}, base
        for _, src, to, dst, halves in plan:
            for h in halves:
                out[dst, h, src] = chan(n, at(src, h), at(dst, h), to)
                n += 1
        return out

    xp, xm, pa = dev(dx=1), dev(dx=3), dev(da=1)
    zp, zm, pb = dev(dz=1), dev(dz=3), dev(db=1)
    sib = dev(dk=1)
    gi = gather(GI, I, 2, IMG, xp, xm, pa)
    gt = gather(GT, T, 1, TXT, zp, zm, pb)
    sb = {
        p: chan(SIB + s, I.at[2 * s * B : (2 * s + 1) * B], I.at[(2 * s + 1) * B : (2 * s + 2) * B], sib)
        for s, p in enumerate(IMG)
    }

    def come(cps, dst, h):
        for (to, half, _), cp in cps.items():
            if (to, half) == (dst, h):
                cp.wait_recv()

    for first in (True, False):
        for dst, hh in (((0, 1), (0, 1)), ((3, 0), (0, 1)), ((1, 0), (1, 0))):
            h = hh[0] if first else hh[1]
            gi[dst, h, (0, 0)].start()
            gt[dst, h, (0, 0)].start()
    sb[0, 0].start()
    MC[...] = jnp.full(MC.shape, -1e30, f32)
    SC[...] = jnp.zeros(SC.shape, f32)
    MS[:, :, 0:B] = jnp.full((8, B, B), -1e30, f32)
    MS[:, :, B : 2 * B] = jnp.zeros((8, B, B), f32)
    ACC[...] = jnp.zeros(ACC.shape, f32)

    def images(i):
        return I[pl.ds(pl.multiple_of(i * 2 * B, 2 * B), 2 * B), :]

    def images(i):
        return I[pl.ds(pl.multiple_of(i * 2 * B, 2 * B), 2 * B), :]

    def logit_tile(i, j):
        return c2 * lax.dot_general(images(i), T[j * B : (j + 1) * B, :], NT, preferred_element_type=f32)

    def lrow(i, e):
        return pl.multiple_of((jnp.minimum(i // 2, KEPT - 1) if e else i // 2) * 2 * B, 2 * B)

    def mm_section(i, jp, e):
        for n in (0, 1):
            j = 2 * jp + n
            xt = logit_tile(i, j)
            L[e][pl.ds(lrow(i, e), 2 * B), j * B : (j + 1) * B] = xt
            top = jnp.maximum(xt[:, :128], xt[:, 128:])
            TM[e][...] = jnp.maximum(TM[e][...], top) if n else top
            CM[e][:, n * B : (n + 1) * B] = jnp.max(xt.reshape(2 * B // 8, 8, B), axis=0)

    def st_section(i, jp, e):
        cols = slice(jp * 2 * B, (jp + 1) * 2 * B)
        old = MC[:, cols]
        mc = jnp.maximum(old, CM[e][...])
        MC[:, cols] = mc
        acc = SC[:, cols] * jnp.exp2(old - mc)
        U = 64
        for q in (0, 1):
            for u in range(B // U):
                l = L[e][pl.ds(lrow(i, e) + q * B + u * U, U), cols]
                rows, mcol, scol = slice(u * U, (u + 1) * U), slice(q * 128, (q + 1) * 128), slice(B + q * 128, B + (q + 1) * 128)
                old = MS[i, rows, mcol]
                m = jnp.maximum(old, TM[e][q * B + u * U : q * B + (u + 1) * U])
                MS[i, rows, mcol] = m
                s = MS[i, rows, scol] * jnp.exp2(old - m)
                for v in range(4):
                    s = s + jnp.exp2(l[:, v * 128 : (v + 1) * 128] - m)
                MS[i, rows, scol] = s
                acc = acc + jnp.sum(jnp.exp2(l.reshape(U // 8, 8, 2 * B) - mc[None]), axis=0)
        SC[:, cols] = acc

    for cps in (gi, gt):
        come(cps, (0, 1), 0)
        cps[(3, 1), 0, (0, 1)].start()
        come(cps, (3, 0), 0)
        cps[(2, 0), 0, (3, 0)].start()
        come(cps, (1, 0), 1)
        cps[(2, 0), 1, (1, 0)].start()
    for cps in (gi, gt):
        come(cps, (0, 1), 1)
        cps[(1, 1), 1, (0, 1)].start()
        come(cps, (3, 0), 1)
        cps[(3, 1), 1, (3, 0)].start()
        come(cps, (1, 0), 0)
        cps[(1, 1), 0, (1, 0)].start()
    sb[0, 1].start()
    sb[3, 0].start()
    sb[1, 0].start()
    for p in ((0, 0), (0, 1), (3, 0), (1, 0)):
        sb[p].wait_recv()

    zero = jnp.int32(0)

    def second():
        for cps in (gi, gt):
            come(cps, (3, 1), 0)
            cps[(2, 1), 0, (3, 1)].start()
            come(cps, (1, 1), 1)
            cps[(2, 1), 1, (1, 1)].start()

    def last():
        for p in ((2, 0), (2, 1)):
            for h in (0, 1):
                come(gi, p, h)
            sb[p].start()
        for p in ((2, 0), (2, 1)):
            for h in (0, 1):
                come(gt, p, h)
        pairs(0, 3, (3,), True)
        sb[2, 0].wait_recv()
        sb[2, 1].wait_recv()

    def pairs(first, count, jps, ahead, before=None):
        end = first + count - 1

        def one(t, carry):
            if before is not None:
                pl.when(t == end)(before)
            ev, od = look_up(t, EVEN), look_up(t, ODD)
            if not ahead:
                mm_section(ev, jps[0], 0)
            for n, jp in enumerate(jps):
                st_section(ev, jp, 0)
                mm_section(od, jp, 1)
                st_section(od, jp, 1)
                if n + 1 < len(jps):
                    mm_section(ev, jps[n + 1], 0)
                elif ahead:
                    mm_section(look_up(jnp.minimum(t + 1, end), EVEN), jps[0], 0)
            return carry

        if ahead:
            mm_section(jnp.int32(EVEN[first]), jps[0], 0)
        lax.fori_loop(first, first + count, one, 0)

    pairs(0, 2, (0, 1), True, second)
    for cps in (gi, gt):
        come(cps, (3, 1), 1)
        come(cps, (1, 1), 0)
    sb[3, 1].start()
    sb[1, 1].start()
    pairs(0, 2, (2,), True)
    sb[3, 1].wait_recv()
    sb[1, 1].wait_recv()
    pairs(2, 2, (0, 1, 2), False, last)
    pairs(3, 1, (3,), False)

    eye = lax.broadcasted_iota(jnp.int32, (128, 128), 0) == lax.broadcasted_iota(jnp.int32, (128, 128), 1)

    def image_block(i, q):
        return ((k + q) % 2) * 8 + ((a + slot_pair(i, IMG)) % 2) * 4 + (x + slot_ring(i, IMG)) % 4

    def text_block(j):
        return ((b + slot_pair(j, TXT)) % 2) * 4 + (z + slot_ring(j, TXT)) % 4

    def row_lse(i, carry):
        for q in (0, 1):
            m = MS[i, :, q * 128 : (q + 1) * 128]
            s = MS[i, :, B + q * 128 : B + (q + 1) * 128]
            mr = jnp.max(m, axis=1, keepdims=True)
            lse = mr + jnp.log2(jnp.sum(s * jnp.exp2(m - mr), axis=1, keepdims=True))
            for h in (0, 1):
                v = jnp.broadcast_to(lse[h * 128 : (h + 1) * 128], (128, 128))
                RSEND[pl.ds(image_block(i, q) * 2 + h, 1), :] = jnp.sum(jnp.where(eye, v, 0.0), axis=0, keepdims=True)
        return carry

    lax.fori_loop(0, 8, row_lse, 0)
    rows_out = []
    for dx, da, dk in row_peers:
        to, here = dk * 8 + da * 4 + dx, dk * 8 + da * 4 + (4 - dx) % 4
        rows_out.append(chan(ROWS + here, RSEND, RRECV.at[here], dev(dx=dx, da=da, dk=dk)))
        rows_out[-1].start()
    mc = MC[...]
    mr = jnp.max(mc, axis=0, keepdims=True)
    lse = mr + jnp.log2(jnp.sum(SC[...] * jnp.exp2(mc - mr), axis=0, keepdims=True))
    for j in range(8):
        for h in (0, 1):
            CSEND[pl.ds(text_block(jnp.int32(j)) * 2 + h, 1), :] = lse[:, j * B + h * 128 : j * B + (h + 1) * 128]
    cols_out = []
    for dz, db in col_peers:
        here = db * 4 + (4 - dz) % 4
        cols_out.append(chan(COLS + here, CSEND, CRECV.at[here], dev(dz=dz, db=db)))
        cols_out[-1].start()

    for cp in cols_out:
        cp.wait_recv()
    parts = [CSEND[...]] + [CRECV[n] for n in range(1, 8)]
    m = functools.reduce(jnp.maximum, parts)
    CLSE[...] = m + 1.0 + jnp.log2(sum(jnp.exp2(v - m) for v in parts))
    for j in range(8):
        for h in (0, 1):
            MC[:, j * B + h * 128 : j * B + (h + 1) * 128] = jnp.broadcast_to(
                CLSE[pl.ds(text_block(jnp.int32(j)) * 2 + h, 1), :], (8, 128)
            )
    for cp in rows_out:
        cp.wait_recv()
    parts = [RSEND[...]] + [RRECV[n] for n in range(1, 16)]
    m = functools.reduce(jnp.maximum, parts)
    RLSE[...] = m + 1.0 + jnp.log2(sum(jnp.exp2(v - m) for v in parts))

    def spread_rows(i, e):
        for q in (0, 1):
            for h in (0, 1):
                v = RLSE[pl.ds(image_block(i, q) * 2 + h, 1), :]
                v = jnp.sum(jnp.where(eye, jnp.broadcast_to(v, (128, 128)), 0.0), axis=1, keepdims=True)
                TM[e][q * B + h * 128 : q * B + (h + 1) * 128] = jnp.broadcast_to(v, (128, 128))

    def grow(i):
        return pl.multiple_of((i // 2) * 2 * B, 2 * B)

    def grads(i, e):
        U = 32
        acc = ACC[...]
        for q in (0, 1):
            for h in (0, 1):
                rl = TM[e][q * B + h * 128 : q * B + (h + 1) * 128]
                for u in range(128 // U):
                    off = q * B + h * 128 + u * U
                    rb = rl[u * U : (u + 1) * U]
                    rb = jnp.concatenate([rb, rb], axis=1)
                    for j in range(8):
                        l = L[e][pl.ds(lrow(i, e) + off, U), j * B : (j + 1) * B]
                        cl = MC[:, j * B : (j + 1) * B]
                        g = jnp.exp2(l - rb) + jnp.exp2(l.reshape(U // 8, 8, B) - cl[None]).reshape(U, B)
                        w = jnp.sum((g * l).reshape(U // 8, 8, B), axis=0)
                        acc = acc + w[:, :128] + w[:, 128:]
                        G[e][pl.ds(grow(i) + off, U), j * B : (j + 1) * B] = g.astype(bf16)
        ACC[...] = acc

    def matched(i, par):
        ai, xi = (a + slot_pair(i, IMG)) % 2, (x + slot_ring(i, IMG)) % 4
        yi = ai + b * (3 - 2 * ai)
        here = (x % 2 == b) & ((z + z // 2) % 2 == a) & (xi % 2 == k)
        j = text_slot((2 * (yi % 2) + xi // 2 - z + 4) % 4, (z // 2 + b) % 2)
        for q in (0, 1):

            @pl.when(here & ((k + q) % 2 == x // 2))
            def _():
                for h in (0, 1):
                    rows = q * B + h * 128
                    cols = pl.ds(pl.multiple_of(j * B + h * 128, 128), 128)
                    l = L[par][pl.ds(lrow(i, par) + rows, 128), cols]
                    g = jnp.exp2(l - TM[par][rows : rows + 128]) + jnp.exp2(l - MC[0:1, cols])
                    g = jnp.where(eye, g - 1.0, g)
                    G[par][pl.ds(grow(i) + rows, 128), cols] = g.astype(bf16)
                    w = jnp.where(eye, l, 0.0)
                    ACC[...] -= jnp.sum(w.reshape(16, 8, 128), axis=0)

    def image_product(i, e):
        p = jnp.dot(G[e][pl.ds(grow(i), 2 * B), :], T[...], preferred_element_type=f32)
        PB[e, 0] = p[:B]
        PB[e, 1] = p[B:]

    def scatter(base, src, own, own_half, fr, xr, ar, ar_half, plus, minus, partner):
        out = {}
        for n, p in enumerate((1, 0)):
            s, lo, hi = base + 6 * n, slice(0, H), slice(H, B)
            out[2, p, 0] = chan(s + 0, src((2, p)).at[lo], fr.at[p, 0], plus)
            out[2, p, 1] = chan(s + 1, src((2, p)).at[hi], fr.at[p, 1], minus)
            out[1, p, 0] = chan(s + 2, src((1, p)).at[lo], xr.at[0, p, lo], plus)
            out[1, p, 1] = chan(s + 3, src((1, p)).at[hi], xr.at[0, p, hi], plus)
            out[3, p, 0] = chan(s + 4, src((3, p)).at[lo], xr.at[1, p, lo], minus)
            out[3, p, 1] = chan(s + 5, src((3, p)).at[hi], xr.at[1, p, hi], minus)
        out[0, 1, 0] = chan(base + 12, own.at[:, 0:W], ar, partner)
        out[0, 1, 1] = chan(base + 13, own_half, ar_half, partner)
        return out

    stage = {(2, 1): 0, (3, 1): 1, (1, 1): 2, (2, 0): 0, (3, 0): 1, (1, 0): 2}
    xs = lambda place: XS.at[stage[place]]
    ts = lambda place: TS.at[stage[place]]
    ltext = lambda s: LE.at[s * B : (s + 1) * B, 0:E]
    ri = scatter(RI, xs, MS.at[1], PS, FR, XR, AR, ARH, xp, xm, pa)
    rt = scatter(RT, ts, ltext(1), PST, FRT, XRT, ART, ARHT, zp, zm, pb)

    def across(i, e):
        return chan(DD + i, PB.at[e, 1], MS.at[i], sib)

    def half(h):
        return pl.ds(h * H, H)

    def free(cps, place):
        if place[1] == 0:
            for h in (0, 1):
                cps[place[0], 1, h].wait_send()

    def send_far(cps, place, p, stage_ref):
        free(cps, place)
        stage_ref[...] = p[...].astype(bf16)
        cps[(*place, 0)].start()
        cps[(*place, 1)].start()

    mixed = {1: 0, 3: 1}

    def send_pure(cps, place, p, stage_ref):
        h = 1 - mixed[place[0]]
        free(cps, place)
        stage_ref[half(h)] = p[half(h)].astype(bf16)
        cps[(*place, h)].start()

    def send_mixed(cps, place, p, stage_ref, fr):
        h = mixed[place[0]]
        cps[2, place[1], h].wait_recv()
        stage_ref[half(h)] = (p[half(h)] + fr[place[1], h].astype(f32)).astype(bf16)
        cps[(*place, h)].start()

    def arrived(cps, pair):
        for ring in (1, 3):
            for h in (0, 1):
                cps[ring, pair, h].wait_recv()

    def send_pair(cps, p, half_ref, xr):
        arrived(cps, 1)
        p[...] += xr[0, 1].astype(f32) + xr[1, 1].astype(f32)
        half_ref[...] = p[:, W:E].astype(bf16)
        cps[0, 1, 0].start()
        cps[0, 1, 1].start()

    def image_sum(s):
        place = IMG[s]
        across(s, s % 2).wait_recv()
        MS[s] += PB[s % 2, 0]
        if place[0] == 2:
            send_far(ri, place, MS.at[s], xs(place))
        elif place[0] % 2:
            send_pure(ri, place, MS.at[s], xs(place))
        across(s, s % 2).wait_send()

    def image_mixed(place):
        send_mixed(ri, place, MS.at[IMG.index(place)], xs(place), FR)

    def again(i):
        for j in range(8):
            L[1][(KEPT - 1) * 2 * B : KEPT * 2 * B, j * B : (j + 1) * B] = logit_tile(i, j)

    def g_half(i, e):
        if e:
            pl.when(i >= 2 * KEPT - 1)(lambda: again(i))
        grads(i, e)
        image_product(i + 1, 1 - e)
        spread_rows(jnp.maximum(i - 1, 0), 1 - e)
        matched(i, e)
        across(i + 1, 1 - e).start()
        for s in range(7, 1, -1):
            if s % 2 == e:

                @pl.when(i + 2 == s)
                def _():
                    image_sum(s)

    def g_step(t, carry):
        g_half(6 - 2 * t, 0)

        @pl.when(t == 2)
        def _():
            image_mixed((3, 1))
            image_mixed((1, 1))

        g_half(5 - 2 * t, 1)
        return carry

    seven = jnp.int32(7)
    spread_rows(seven, 1)
    grads(seven, 1)
    spread_rows(seven - 1, 0)
    matched(seven, 1)
    lax.fori_loop(0, 3, g_step, 0)
    g_half(zero, 0)

    sc1_out = []
    mine = image_block(zero, 0)
    SR1[mine] = ACC[...]
    for dx, da, dk in row_peers:
        here = dk * 8 + da * 4 + (4 - dx) % 4
        sc1_out.append(chan(SC1 + here, ACC, SR1.at[mine], dev(dx=dx, da=da, dk=dk)))

    mine_t = text_block(zero)
    sc2_out = [
        chan(SC2 + db * 4 + (4 - dz) % 4, ACC, SR2.at[mine_t], dev(dz=dz, db=db)) for dz, db in col_peers
    ]

    def text_send(kind, place, *more):
        kind(rt, place, ltext(TXT.index(place)), ts(place), *more)

    def text_step(t, carry):
        j = look_up(t, TEXT_ORDER)
        cols = pl.ds(pl.multiple_of(j * B, B), B)
        p = None
        for s in range(8):
            v = lax.dot_general(
                G[s % 2][(s // 2) * 2 * B : (s // 2 + 1) * 2 * B, cols],
                I[s * 2 * B : (s + 1) * 2 * B, :],
                TN, preferred_element_type=f32,
            )
            p = v if p is None else p + v
        LE[pl.ds(pl.multiple_of(j * B, B), B), 0:E] = p

        @pl.when(t == 0)
        def _():
            text_send(send_far, (2, 1))

        @pl.when(t == 1)
        def _():
            text_send(send_pure, (3, 1))

        @pl.when(t == 2)
        def _():
            text_send(send_pure, (1, 1))

        @pl.when(t == 3)
        def _():
            text_send(send_mixed, (3, 1), FRT)
            text_send(send_mixed, (1, 1), FRT)
            text_send(send_far, (2, 0))
            image_sum(1)
            send_pair(ri, MS.at[1], PS, XR)
            image_mixed((3, 0))
            image_mixed((1, 0))

        @pl.when(t == 4)
        def _():
            text_send(send_pure, (3, 0))
            image_product(zero, 0)
            across(zero, 0).start()
            for cp in sc1_out:
                cp.start()

        @pl.when(t == 5)
        def _():
            text_send(send_pure, (1, 0))

        @pl.when(t == 6)
        def _():
            image_sum(0)
            for cp in [*gi.values(), *gt.values(), *sb.values(), *rows_out, *cols_out]:
                cp.wait_send()

        @pl.when(t == 7)
        def _():
            send_pair(rt, ltext(1), PST, XRT)
            text_send(send_mixed, (3, 0), FRT)
            text_send(send_mixed, (1, 0), FRT)
            for cp in sc1_out:
                cp.wait()
            ACC[...] = sum(SR1[n] for n in range(16))
            SR2[mine_t] = ACC[...]
            for cp in sc2_out:
                cp.start()

        return carry

    lax.fori_loop(0, 8, text_step, 0)

    def finish(cps, p, xr, ar, ar_half, out, sem):
        arrived(cps, 0)
        p[...] += xr[0, 0].astype(f32) + xr[1, 0].astype(f32)
        cps[0, 1, 0].wait_recv()
        cps[0, 1, 1].wait_recv()
        p[:, 0:W] += ar[...]
        p[:, W:E] += ar_half[...].astype(f32)
        store = pltpu.make_async_copy(p, out, sem)
        store.start()
        return store

    for cp in sc2_out:
        cp.wait()
    gs_ref[0, 0] = jnp.sum(sum(SR2[n] for n in range(8))) / c2
    store_i = finish(ri, MS.at[0], XR, AR, ARH, out_hbm.at[0], LS.at[0])
    store_t = finish(rt, ltext(0), XRT, ART, ARHT, out_hbm.at[1], LS.at[1])

    for cps in (ri, rt):
        for (ring, pair, _), cp in cps.items():
            if ring == 0 or pair == 0:
                cp.wait_send()
    store_i.wait()
    store_t.wait()


def on_device(image_embeds, text_embeds, logit_scale):
    f32, bf16 = jnp.float32, jnp.bfloat16
    any_space = pl.BlockSpec(memory_space=pl.ANY)
    smem = pl.BlockSpec(memory_space=pltpu.SMEM)
    grads, grad_scale = pl.pallas_call(
        kernel,
        out_shape=(
            jax.ShapeDtypeStruct((2, B, E), f32),
            jax.ShapeDtypeStruct((1, 1), f32),
        ),
        in_specs=[smem, any_space, any_space],
        out_specs=(any_space, smem),
        scratch_shapes=[
            pltpu.VMEM((16 * B, E), bf16),
            pltpu.VMEM((8 * B, E), bf16),
            pltpu.VMEM((8 * B, 8 * B), f32),
            pltpu.VMEM((KEPT * 2 * B, 8 * B), f32),
            pltpu.VMEM((2 * B, 128), f32),
            pltpu.VMEM((2 * B, 128), f32),
            pltpu.VMEM((8, 2 * B), f32),
            pltpu.VMEM((8, 2 * B), f32),
            pltpu.VMEM((8 * B, 8 * B), bf16),
            pltpu.VMEM((8 * B, 8 * B), bf16),
            pltpu.VMEM((8, B, E), f32),
            pltpu.VMEM((2, 2, B, E), f32),
            pltpu.VMEM((3, B, E), bf16),
            pltpu.VMEM((3, B, E), bf16),
            pltpu.VMEM((B, E - W), bf16),
            pltpu.VMEM((B, E - W), bf16),
            pltpu.VMEM((2, 2, H, E), bf16),
            pltpu.VMEM((2, 2, B, E), bf16),
            pltpu.VMEM((B, W), f32),
            pltpu.VMEM((B, E - W), bf16),
            pltpu.VMEM((2, 2, H, E), bf16),
            pltpu.VMEM((2, 2, B, E), bf16),
            pltpu.VMEM((B, W), f32),
            pltpu.VMEM((B, E - W), bf16),
            pltpu.VMEM((8, 8 * B), f32),
            pltpu.VMEM((8, 8 * B), f32),
            pltpu.VMEM((32, 128), f32),
            pltpu.VMEM((16, 32, 128), f32),
            pltpu.VMEM((16, 128), f32),
            pltpu.VMEM((8, 16, 128), f32),
            pltpu.VMEM((32, 128), f32),
            pltpu.VMEM((16, 128), f32),
            pltpu.VMEM((8, 128), f32),
            pltpu.VMEM((16, 8, 128), f32),
            pltpu.VMEM((8, 8, 128), f32),
            pltpu.SemaphoreType.DMA((CHANNELS,)),
            pltpu.SemaphoreType.DMA((CHANNELS,)),
            pltpu.SemaphoreType.DMA((2,)),
        ],
        compiler_params=pltpu.CompilerParams(
            collective_id=0, has_side_effects=True, vmem_limit_bytes=64 << 20
        ),
        cost_estimate=pl.CostEstimate(flops=6 * 4096 * 2048 * 512, bytes_accessed=4 << 20, transcendentals=4 * 4096 * 2048),
    )(logit_scale.reshape(1), image_embeds, text_embeds)
    return logit_scale * grads[0], logit_scale * grads[1], grad_scale.reshape(())


def solution(mesh):
    return jax.shard_map(
        on_device,
        mesh=mesh,
        in_specs=(P(("row", "col"), None), P(("col", "row"), None), P()),
        out_specs=(P(("row", "col"), None), P(("col", "row"), None), P()),
        check_vma=False,
    )
```
